256 devices in a mesh: dp: 32 (over z, x), gen: 8 (over y, core).
Axes of the slice: x: 4, y: 4, z: 8, core: 2. Of those that a mesh axis runs over, the one named last changes fastest.
Arguments:
- private: bfloat16 [32768, 1024], P('dp', 'gen'), may hold values from -12 to 12, as said below
- generated: bfloat16 [16384, 1024], P(('gen', 'dp')), may hold values from -12 to 12, as said below
- noise: float32 [16384, 1024], P(('gen', 'dp')), may hold values from -3 to 3
Outputs:
- update: float32 [16384, 1024], P(('gen', 'dp'))
The draws below stay inside these ranges and needn't reach their ends.
Inputs may be any that keep to these rules, and one draw needn't show every extreme that they name: `private`: private embeddings, drawn from a seed. `generated`: generated embeddings, drawn from a seed.
All inputs are finite; a program needn't handle non-finite values.
Results may differ from the reference program's by a relative error of at most 0.0024.
Values may be sent and summed in bfloat16 or wider, within the bound.
No kernel may reach another device: no remote copies, remote signals or barrier semaphores. Data moves between devices by JAX's collectives and lax.ppermute only.
A program may use at most 64 MiB of HBM per device.

```python
import math
import jax
import jax.numpy as jnp
from jax import lax

D = 1024
PRIV_DEV = 1024
ITERS = 3
NP = 32768
NG = 16384
N_DP = 32


def shared_generated(key, low, high, paired):
    key = jax.random.fold_in(key, 101)
    base = jnp.clip(jax.random.normal(jax.random.fold_in(key, 1), (NG, D), jnp.float32), -5.0, 5.0)
    scales = jax.random.uniform(jax.random.fold_in(key, 2), (NG, 1), jnp.float32, low, high)
    jitter = 0.2 * jnp.clip(jax.random.normal(jax.random.fold_in(key, 3), (NG, D), jnp.float32), -5.0, 5.0)
    indices = jnp.arange(NG)[:, None]
    partner_rows = (indices % 2 == 1) & (indices < paired)
    base = jnp.where(partner_rows, jnp.roll(base, 1, axis=0) + jitter, base)
    scales = jnp.where(partner_rows, jnp.roll(scales, 1, axis=0), scales)
    return base * scales


def draw_generated(key, part):
    values = shared_generated(key, 1.0, 1.0, 0)
    return values.astype(jnp.bfloat16)


def draw_private(key, part):
    key = jax.random.fold_in(key, 7)
    values = jnp.clip(jax.random.normal(key, (NP, D), jnp.float32), -5.0, 5.0)
    return values.astype(jnp.bfloat16)


def block_scale(key, shape, cuts, low, largest):
    def one(axis_at, shards_of):
        draws = jax.random.uniform(jax.random.fold_in(jax.random.fold_in(key, 6), axis_at), (shards_of,), jnp.float32, low / len(cuts), largest / len(cuts))
        return jnp.repeat(jnp.exp(draws), shape[axis_at] // shards_of).reshape((-1,) + (1,) * (len(shape) - axis_at - 1))

    loudness = one(*cuts[0])
    for cut in cuts[1:]:
        loudness = loudness * one(*cut)
    return loudness


def normal_values(key, dims, spread, limit, shards=(), kind=jnp.bfloat16):
    factor_of = block_scale(key, dims, shards, -0.22, 0.18) if shards else 1.0
    array = jax.random.normal(key, dims, jnp.float32) * spread * factor_of
    return jnp.minimum(jnp.maximum(array, -limit), limit).astype(kind)


def setup_inputs(seed: int = 0) -> dict:
    arg_keys = jax.random.split(jax.random.key(seed), 4)
    return {
        "private": draw_private(jax.random.fold_in(arg_keys[3], 71), 0),
        "generated": draw_generated(jax.random.fold_in(arg_keys[3], 71), 0),
        "noise": normal_values(arg_keys[2], (NG, D), 0.5, 3.0, ((0, 256),), jnp.float32),
    }


smoothing_epsilon = 0.02


def block_costs(private_block, private_sq, generated, generated_sq):
    cross = jnp.dot(private_block, generated.T, preferred_element_type=jnp.float32)
    return (private_sq[:, None] + generated_sq[None, :] - 2.0 * cross) / D


def reference(private, generated, noise):
    private_blocks = private.reshape(N_DP, PRIV_DEV, D)
    private_sq = jnp.sum(private.astype(jnp.float32) ** 2, axis=1).reshape(N_DP, PRIV_DEV)
    generated_sq = jnp.sum(generated.astype(jnp.float32) ** 2, axis=1)
    source_mass_logarithm = math.log(NP)
    target_mass_logarithm = math.log(NG)

    def sweep(target_lagrange_vector):
        def step(carry, block):
            target_current_maximal, target_accrued_amount = carry
            private_block, block_sq = block
            distance_grid = block_costs(private_block, block_sq, generated, generated_sq)
            kernel_grid = (target_lagrange_vector[None, :] - distance_grid) / smoothing_epsilon
            maximal_element = jnp.max(kernel_grid, axis=1)
            accumulated_exponential = jnp.sum(jnp.exp(kernel_grid - maximal_element[:, None]), axis=1)
            source_lagrange_vector = -smoothing_epsilon * (maximal_element + jnp.log(accumulated_exponential) - target_mass_logarithm)
            target_kernel_grid = (source_lagrange_vector[:, None] - distance_grid) / smoothing_epsilon
            newtop = jnp.maximum(target_current_maximal, jnp.max(target_kernel_grid, axis=0))
            target_accrued_amount = target_accrued_amount * jnp.exp(target_current_maximal - newtop) + jnp.sum(jnp.exp(target_kernel_grid - newtop[None, :]), axis=0)
            return (newtop, target_accrued_amount), source_lagrange_vector

        start = (jnp.full((NG,), -jnp.inf, jnp.float32), jnp.zeros((NG,), jnp.float32))
        (target_current_maximal, target_accrued_amount), source_lagrange_vector = lax.scan(step, start, (private_blocks, private_sq))
        target_lagrange_vector = -smoothing_epsilon * (target_current_maximal + jnp.log(target_accrued_amount) - source_mass_logarithm)
        return source_lagrange_vector, target_lagrange_vector

    target_lagrange_vector = jnp.zeros((NG,), jnp.float32)
    for step_index in range(ITERS):
        source_lagrange_vector, target_lagrange_vector = sweep(target_lagrange_vector)

    def accumulate(barycenter, block):
        private_block, block_sq, lagrange_segment = block
        distance_grid = block_costs(private_block, block_sq, generated, generated_sq)
        coupling_plan = jnp.exp((lagrange_segment[:, None] + target_lagrange_vector[None, :] - distance_grid) / smoothing_epsilon - source_mass_logarithm)
        coupling_plan = coupling_plan.astype(jnp.bfloat16)
        return barycenter + jnp.dot(coupling_plan.T, private_block, preferred_element_type=jnp.float32), None

    barycenter, unused = lax.scan(accumulate, jnp.zeros((NG, D), jnp.float32), (private_blocks, private_sq, source_lagrange_vector))
    return generated.astype(jnp.float32) - barycenter + noise
```

```python
import functools
import math

import jax
import jax.numpy as jnp
from jax import lax
from jax.experimental import pallas as pl
from jax.experimental.pallas import tpu as pltpu
from jax.sharding import Mesh
from jax.sharding import PartitionSpec as P


EPS = 0.02
F32 = jnp.float32
BF16 = jnp.bfloat16
F16 = jnp.float16
LANES = 128
SUB = 64


def to_rows(column):
    flat = jnp.transpose(column)[0:1, :]
    return jnp.concatenate(
        [flat[:, q * LANES:(q + 1) * LANES] for q in range(column.shape[0] // LANES)], axis=0
    )


def sum_to_rows(lanes):
    flat = jnp.sum(jnp.transpose(lanes), axis=0, keepdims=True)
    return jnp.concatenate(
        [flat[:, q * LANES:(q + 1) * LANES] for q in range(lanes.shape[0] // LANES)], axis=0
    )


def to_columns(rows, out_ref):
    for q in range(rows.shape[0]):
        out_ref[q * LANES:(q + 1) * LANES, :] = jnp.transpose(
            jnp.broadcast_to(rows[q:q + 1, :], (LANES, LANES))
        )


def logsumexp0(x):
    top = jnp.max(x, axis=0)
    return top + jnp.log(jnp.sum(jnp.exp(x - top[None]), axis=0))


def score_kernel(scale, p_ref, g_ref, t_ref, l_ref, c0_ref, rows_ref):
    step = pl.program_id(0)
    tiles = t_ref.shape[0]

    @pl.when(step == 0)
    def _():
        g = g_ref[...].astype(F32)
        sq = jnp.sum(g * g, axis=1, keepdims=True)
        c0_ref[...] = jnp.broadcast_to(sq * (-0.5 * scale), c0_ref.shape)

    p = jnp.concatenate([p_ref[0, f] for f in range(p_ref.shape[1])], axis=1)
    cross = lax.dot_general(g_ref[...], p, (((1,), (1,)), ((), ())), preferred_element_type=F32)
    for k in range(tiles):
        t = cross[:, k * LANES:(k + 1) * LANES] * scale + c0_ref[...]
        t_ref[k] = t
        top = jnp.max(t, axis=0, keepdims=True)
        rows_ref[pl.ds(step * tiles + k, 1), :] = top + jnp.log(
            jnp.sum(jnp.exp(t - top), axis=0, keepdims=True)
        )

    @pl.when(step == pl.num_programs(0) - 1)
    def _():
        l_ref[...] = jnp.broadcast_to(rows_ref[...][None], l_ref.shape)


def first_column_kernel(log_ng, l_ref, t_ref, r_ref, lc_ref, m_ref, s_ref):
    step = pl.program_id(0)
    tiles = t_ref.shape[0]

    @pl.when(step == 0)
    def _():
        r_ref[...] = log_ng - logsumexp0(l_ref[...])
        m_ref[...] = jnp.full(m_ref.shape, -1e38, F32)
        s_ref[...] = jnp.zeros(s_ref.shape, F32)

    r = [r_ref[pl.ds(step * tiles + k, 1), :] for k in range(tiles)]

    @pl.loop(0, m_ref.shape[0], step=SUB)
    def _(c):
        at = pl.ds(pl.multiple_of(c, SUB), SUB)
        u = [t_ref[k, at, :] + r[k] for k in range(tiles)]
        old = m_ref[at, :]
        top = old
        for k in range(tiles):
            top = jnp.maximum(top, u[k])
        s = s_ref[at, :] * jnp.exp(old - top)
        for k in range(tiles):
            s = s + jnp.exp(u[k] - top)
        m_ref[at, :] = top
        s_ref[at, :] = s

    @pl.when(step == pl.num_programs(0) - 1)
    def _():
        m = m_ref[...]
        top = jnp.max(m, axis=1, keepdims=True)
        total = jnp.sum(s_ref[...] * jnp.exp(m - top), axis=1, keepdims=True)
        lc = to_rows(jnp.broadcast_to(top + jnp.log(total), m.shape))
        lc_ref[...] = jnp.broadcast_to(lc[None], lc_ref.shape)


def plan_kernel(log_np, lc_ref, r_ref, t_ref, k_ref, rho_ref, c_ref, rows_ref):
    step = pl.program_id(0)
    tiles = t_ref.shape[0]

    @pl.when(step == 0)
    def _():
        to_columns(log_np - logsumexp0(lc_ref[...]), c_ref)

    for k in range(tiles):
        r = r_ref[pl.ds(step * tiles + k, 1), :]

        def body(i, total, k=k, r=r):
            at = pl.ds(pl.multiple_of(i * SUB, SUB), SUB)
            value = jnp.exp(t_ref[k, at, :] + (r + c_ref[at, :]))
            k_ref[k, at, :] = value
            return total + jnp.sum(value.reshape(SUB // 8, 8, LANES), axis=0)

        total = lax.fori_loop(0, c_ref.shape[0] // SUB, body, jnp.zeros((8, LANES), F32), unroll=2)
        rows_ref[pl.ds(step * tiles + k, 1), :] = jnp.sum(total, axis=0, keepdims=True)

    @pl.when(step == pl.num_programs(0) - 1)
    def _():
        rho_ref[...] = jnp.broadcast_to(rows_ref[...][None], rho_ref.shape)


def column_sum_kernel(ng, rho_ref, k_ref, sums_ref, u_ref, acc_ref):
    step = pl.program_id(0)
    tiles = k_ref.shape[0]

    @pl.when(step == 0)
    def _():
        u_ref[...] = ng / jnp.sum(rho_ref[...], axis=0)
        acc_ref[...] = jnp.zeros(acc_ref.shape, F32)

    u = [u_ref[pl.ds(step * tiles + k, 1), :] for k in range(tiles)]

    @pl.loop(0, acc_ref.shape[0], step=SUB)
    def _(c):
        at = pl.ds(pl.multiple_of(c, SUB), SUB)
        total = acc_ref[at, :]
        for k in range(tiles):
            total = total + k_ref[k, at, :] * u[k]
        acc_ref[at, :] = total

    @pl.when(step == pl.num_programs(0) - 1)
    def _():
        sums_ref[...] = jnp.broadcast_to(sum_to_rows(acc_ref[...])[None], sums_ref.shape)


def row_sum_kernel(np_, sums_ref, k_ref, v_ref, rho_ref, rows_ref):
    step = pl.program_id(0)
    tiles = k_ref.shape[0]

    @pl.when(step == 0)
    def _():
        to_columns(np_ / jnp.sum(sums_ref[...], axis=0), v_ref)

    def body(i, totals):
        at = pl.ds(pl.multiple_of(i * SUB, SUB), SUB)
        v = v_ref[at, :]
        return tuple(
            totals[k] + jnp.sum((k_ref[k, at, :] * v).reshape(SUB // 8, 8, LANES), axis=0)
            for k in range(tiles)
        )

    totals = lax.fori_loop(
        0, v_ref.shape[0] // SUB, body, tuple(jnp.zeros((8, LANES), F32) for _ in range(tiles))
    )
    for k in range(tiles):
        rows_ref[pl.ds(step * tiles + k, 1), :] = jnp.sum(totals[k], axis=0, keepdims=True)

    @pl.when(step == pl.num_programs(0) - 1)
    def _():
        rho_ref[...] = jnp.broadcast_to(rows_ref[...][None], rho_ref.shape)


def barycenter_kernel(ng, rho_ref, v_ref, k_ref, p_ref, out_ref, u_ref, mass_ref, acc_ref, w_ref):
    step = pl.program_id(0)
    tiles = k_ref.shape[0]

    @pl.when(step == 0)
    def _():
        u_ref[...] = ng / jnp.sum(rho_ref[...], axis=0)
        mass_ref[...] = jnp.zeros(mass_ref.shape, F32)
        acc_ref[...] = jnp.zeros(acc_ref.shape, F32)

    u = [u_ref[pl.ds(step * tiles + k, 1), :] for k in range(tiles)]

    @pl.loop(0, mass_ref.shape[0], step=SUB)
    def _(c):
        at = pl.ds(pl.multiple_of(c, SUB), SUB)
        v = v_ref[at, :]
        total = mass_ref[at, :]
        for k in range(tiles):
            w = k_ref[k, at, :] * u[k] * v
            total = total + w
            w_ref[at, k * LANES:(k + 1) * LANES] = w.astype(BF16)
        mass_ref[at, :] = total

    p = jnp.concatenate([p_ref[0, f] for f in range(p_ref.shape[1])], axis=1)
    acc_ref[...] += jnp.dot(w_ref[...], p, preferred_element_type=F32)

    @pl.when(step == pl.num_programs(0) - 1)
    def _():
        owners = out_ref.shape[0]
        rows = acc_ref.shape[0] // owners
        blocks = acc_ref.shape[1] // LANES
        mass = jnp.maximum(jnp.sum(mass_ref[...], axis=1, keepdims=True), 1e-30)
        inverse = jnp.broadcast_to(1.0 / mass, mass_ref.shape)
        log_mass = jnp.transpose(jnp.broadcast_to(jnp.log(mass), mass_ref.shape))[0:1, :]
        for z in range(owners):
            at = slice(z * rows, (z + 1) * rows)
            for q in range(blocks):
                out_ref[z, q * rows:(q + 1) * rows, :] = (
                    acc_ref[at, q * LANES:(q + 1) * LANES] * inverse[at, :]
                )
            part = jnp.concatenate([log_mass[:, at]] * (LANES // rows), axis=1)
            high = jnp.round(part * 16.0) * 0.0625
            low = part - high
            tail = jnp.concatenate([high] * 8 + [low] * 8, axis=0)
            out_ref[z, blocks * rows:, :] = tail


def update_kernel(parts_ref, g_ref, n_ref, out_ref):
    sources = parts_ref.shape[0]
    rows = g_ref.shape[0]
    blocks = g_ref.shape[1] // LANES
    at = blocks * rows
    logs = jnp.concatenate(
        [parts_ref[d, at:at + 1, :] + parts_ref[d, at + 8:at + 9, :] for d in range(sources)], axis=0
    )
    weights = jnp.exp(logs - jnp.max(logs, axis=0, keepdims=True))
    weights = weights / jnp.sum(weights, axis=0, keepdims=True)
    columns = [
        jnp.transpose(jnp.broadcast_to(weights[d:d + 1, :], (LANES, LANES)))[0:rows, :]
        for d in range(sources)
    ]
    for q in range(blocks):
        lanes = slice(q * LANES, (q + 1) * LANES)
        total = parts_ref[0, q * rows:(q + 1) * rows, :] * columns[0]
        for d in range(1, sources):
            total = total + parts_ref[d, q * rows:(q + 1) * rows, :] * columns[d]
        out_ref[:, lanes] = g_ref[:, lanes].astype(F32) - total + n_ref[:, lanes]


def whole(shape):
    return pl.BlockSpec(shape, lambda b: (0,) * len(shape))


def shards(private, generated, noise):
    rows_per, width = private.shape
    own, features = generated.shape
    nz, nx = lax.axis_size("z"), lax.axis_size("x")
    peers = ("x", "y", "core")
    n_peers = lax.axis_size(peers)
    cols = own * nz
    rows = rows_per * nx
    np_ = rows * nz
    ng = cols * n_peers
    scale = 2.0 / (features * EPS)
    row_tiles = rows // LANES
    col_tiles = cols // LANES
    tiles = 4
    steps = row_tiles // tiles
    block = tiles * LANES
    per = rows_per // block

    p = lax.all_gather(private, peers, axis=0, tiled=False)
    p = p.reshape(nx, n_peers // nx, rows_per, width)
    g = jnp.broadcast_to(generated[None], (nz, own, features))
    g = lax.all_to_all(g, "z", 0, 0, tiled=True).reshape(cols, features)

    params = pltpu.CompilerParams(
        dimension_semantics=("arbitrary",), vmem_limit_bytes=32 * 1024 * 1024
    )
    p_spec = pl.BlockSpec(
        (1, n_peers // nx, block, width), lambda b: (b // per, 0, b % per, 0)
    )
    t_spec = pl.BlockSpec((tiles, cols, LANES), lambda b: (b, 0, 0))
    t_shape = jax.ShapeDtypeStruct((row_tiles, cols, LANES), F32)
    row_shape = (n_peers, row_tiles, LANES)
    col_shape = (nz, col_tiles, LANES)
    row_out = jax.ShapeDtypeStruct(row_shape, F32)
    col_out = jax.ShapeDtypeStruct(col_shape, F32)
    rows_scratch = pltpu.VMEM((row_tiles, LANES), F32)
    cols_scratch = pltpu.VMEM((cols, LANES), F32)

    def over_peers(a):
        return lax.all_to_all(a, peers, 0, 0, tiled=True)

    def over_z(a):
        return lax.all_to_all(a, "z", 0, 0, tiled=True)

    t, lr = pl.pallas_call(
        functools.partial(score_kernel, scale),
        grid=(steps,),
        in_specs=[p_spec, whole((cols, features))],
        out_specs=[t_spec, whole(row_shape)],
        out_shape=[t_shape, row_out],
        scratch_shapes=[cols_scratch, rows_scratch],
        compiler_params=params,
        name="scores",
    )(p, g)
    lr = over_peers(lr)

    r, lc = pl.pallas_call(
        functools.partial(first_column_kernel, math.log(ng)),
        grid=(steps,),
        in_specs=[whole(row_shape), t_spec],
        out_specs=[whole((row_tiles, LANES)), whole(col_shape)],
        out_shape=[jax.ShapeDtypeStruct((row_tiles, LANES), F32), col_out],
        scratch_shapes=[cols_scratch, cols_scratch],
        compiler_params=params,
        name="first_columns",
    )(lr, t)
    lc = over_z(lc)

    k, rho = pl.pallas_call(
        functools.partial(plan_kernel, math.log(np_)),
        grid=(steps,),
        in_specs=[whole(col_shape), whole((row_tiles, LANES)), t_spec],
        out_specs=[t_spec, whole(row_shape)],
        out_shape=[t_shape, row_out],
        scratch_shapes=[cols_scratch, rows_scratch],
        compiler_params=params,
        name="plan",
    )(lc, r, t)
    rho = over_peers(rho)

    sums = pl.pallas_call(
        functools.partial(column_sum_kernel, float(ng)),
        grid=(steps,),
        in_specs=[whole(row_shape), t_spec],
        out_specs=whole(col_shape),
        out_shape=col_out,
        scratch_shapes=[rows_scratch, cols_scratch],
        compiler_params=params,
        name="column_sums",
    )(rho, k)
    sums = over_z(sums)

    v, rho = pl.pallas_call(
        functools.partial(row_sum_kernel, float(np_)),
        grid=(steps,),
        in_specs=[whole(col_shape), t_spec],
        out_specs=[whole((cols, LANES)), whole(row_shape)],
        out_shape=[jax.ShapeDtypeStruct((cols, LANES), F32), row_out],
        scratch_shapes=[rows_scratch],
        compiler_params=params,
        name="row_sums",
    )(sums, k)
    rho = over_peers(rho)

    part_shape = (nz, own * (features // LANES) + 16, LANES)
    parts = pl.pallas_call(
        functools.partial(barycenter_kernel, float(ng)),
        grid=(steps,),
        in_specs=[whole(row_shape), whole((cols, LANES)), t_spec, p_spec],
        out_specs=whole(part_shape),
        out_shape=jax.ShapeDtypeStruct(part_shape, F32),
        scratch_shapes=[
            rows_scratch,
            cols_scratch,
            pltpu.VMEM((cols, features), F32),
            pltpu.VMEM((cols, block), BF16),
        ],
        compiler_params=params,
        name="barycenter",
    )(rho, v, k, p)
    parts = over_z(parts.astype(F16)).astype(F32)

    return pl.pallas_call(
        update_kernel,
        out_shape=jax.ShapeDtypeStruct((own, features), F32),
        compiler_params=pltpu.CompilerParams(vmem_limit_bytes=32 * 1024 * 1024),
        name="update",
    )(parts, generated, noise)


def solution(mesh):
    fine = Mesh(mesh.devices.reshape(8, 4, 4, 2), ("z", "x", "y", "core"))
    in_specs = (
        P(("z", "x"), ("y", "core")),
        P(("y", "core", "z", "x"), None),
        P(("y", "core", "z", "x"), None),
    )
    out_specs = P(("y", "core", "z", "x"), None)
    return jax.shard_map(shards, mesh=fine, in_specs=in_specs, out_specs=out_specs, check_vma=False)
```

```python
import functools
import itertools
import math

import jax
import jax.numpy as jnp
from jax import lax
from jax.experimental import pallas as pl
from jax.experimental.pallas import tpu as pltpu
from jax.sharding import Mesh
from jax.sharding import PartitionSpec as P


EPS = 0.02
F32 = jnp.float32
BF16 = jnp.bfloat16
F16 = jnp.float16
LANES = 128
SUB = 64


def to_rows(column):
    flat = jnp.transpose(column)[0:1, :]
    return jnp.concatenate(
        [flat[:, q * LANES:(q + 1) * LANES] for q in range(column.shape[0] // LANES)], axis=0
    )


def sum_to_rows(lanes):
    flat = jnp.sum(jnp.transpose(lanes), axis=0, keepdims=True)
    return jnp.concatenate(
        [flat[:, q * LANES:(q + 1) * LANES] for q in range(lanes.shape[0] // LANES)], axis=0
    )


def to_columns(rows, out_ref):
    for q in range(rows.shape[0]):
        out_ref[q * LANES:(q + 1) * LANES, :] = jnp.transpose(
            jnp.broadcast_to(rows[q:q + 1, :], (LANES, LANES))
        )


def logsumexp0(x):
    top = jnp.max(x, axis=0)
    return top + jnp.log(jnp.sum(jnp.exp(x - top[None]), axis=0))


def score_kernel(scale, *refs):
    blocks, (own_ref, far_ref, near_ref, swapped_ref) = refs[:8], refs[8:12]
    p_ref, t_ref, l_ref, g_ref, c0_ref, rows_ref = refs[12:]
    step = pl.program_id(0)
    nx, slices, rows, width = p_ref.shape
    ny = slices // 2
    nz = 8
    x, y, z, core = (lax.axis_index(a) for a in ("x", "y", "z", "core"))
    tiles = t_ref.shape[0]

    @pl.when(step == 0)
    def _():
        first = ((0, -1), (1, -2))
        for ref, pair, second in zip(blocks, (0, 1, 0, 0, 1, 1, 0, 1), (0, 0, -1, 1, -1, 1, -2, 2)):
            for n in range(2):
                a, b = first[pair][n], second
                px = lax.rem(x + jnp.where(core == 0, a, b) + nx, nx)
                py = lax.rem(y + jnp.where(core == 0, b, a) + ny, ny)
                for f in range(2):
                    p_ref[px, 2 * py + f] = ref[n, f]

        own = g_ref.shape[0] // (2 * nz)

        def put(ref, at, k):
            pz = lax.rem(z + k + nz, nz)
            for c in range(2):
                g_ref[pl.ds(pl.multiple_of((c * nz + pz) * own, own), own), :] = ref[at + (c,)]

        sign = jnp.where(core == 0, -1, 1)
        put(own_ref, (), 0)
        put(far_ref, (), 4)
        for k in range(1, 4):
            put(near_ref, (k - 1,), sign * k)
            put(swapped_ref, (k - 1,), -sign * k)

        def squares(i, carry):
            at = pl.ds(pl.multiple_of(i * LANES, LANES), LANES)
            g = g_ref[at, :].astype(F32)
            sq = jnp.sum(g * g, axis=1, keepdims=True)
            c0_ref[at, :] = jnp.broadcast_to(sq * (-0.5 * scale), (LANES, LANES))
            return carry

        lax.fori_loop(0, g_ref.shape[0] // LANES, squares, 0)

    for half in range(2):
        at = slice(half * rows // 2, (half + 1) * rows // 2)
        p = jnp.concatenate([p_ref[step, f, at, :] for f in range(slices)], axis=1)
        cross = lax.dot_general(g_ref[...], p, (((1,), (1,)), ((), ())), preferred_element_type=F32)
        for n in range(tiles // 2):
            k = half * (tiles // 2) + n
            t = cross[:, n * LANES:(n + 1) * LANES] * scale + c0_ref[...]
            t_ref[k] = t
            top = jnp.max(t, axis=0, keepdims=True)
            rows_ref[pl.ds(step * tiles + k, 1), :] = top + jnp.log(
                jnp.sum(jnp.exp(t - top), axis=0, keepdims=True)
            )

    @pl.when(step == pl.num_programs(0) - 1)
    def _():
        l_ref[...] = jnp.broadcast_to(rows_ref[...][None], l_ref.shape)


def first_column_kernel(log_ng, l_ref, t_ref, r_ref, lc_ref, m_ref, s_ref):
    step = pl.program_id(0)
    tiles = t_ref.shape[0]

    @pl.when(step == 0)
    def _():
        r_ref[...] = log_ng - logsumexp0(l_ref[...])
        m_ref[...] = jnp.full(m_ref.shape, -1e38, F32)
        s_ref[...] = jnp.zeros(s_ref.shape, F32)

    r = [r_ref[pl.ds(step * tiles + k, 1), :] for k in range(tiles)]

    @pl.loop(0, m_ref.shape[0], step=SUB)
    def _(c):
        at = pl.ds(pl.multiple_of(c, SUB), SUB)
        u = [t_ref[k, at, :] + r[k] for k in range(tiles)]
        old = m_ref[at, :]
        top = old
        for k in range(tiles):
            top = jnp.maximum(top, u[k])
        s = s_ref[at, :] * jnp.exp(old - top)
        for k in range(tiles):
            s = s + jnp.exp(u[k] - top)
        m_ref[at, :] = top
        s_ref[at, :] = s

    @pl.when(step == pl.num_programs(0) - 1)
    def _():
        m = m_ref[...]
        top = jnp.max(m, axis=1, keepdims=True)
        total = jnp.sum(s_ref[...] * jnp.exp(m - top), axis=1, keepdims=True)
        lc = to_rows(jnp.broadcast_to(top + jnp.log(total), m.shape))
        lc_ref[...] = jnp.broadcast_to(lc[None], lc_ref.shape)


def plan_kernel(log_np, lc_ref, r_ref, t_ref, k_ref, rho_ref, c_ref, rows_ref):
    step = pl.program_id(0)
    tiles = t_ref.shape[0]

    @pl.when(step == 0)
    def _():
        to_columns(log_np - logsumexp0(lc_ref[...]), c_ref)

    for k in range(tiles):
        r = r_ref[pl.ds(step * tiles + k, 1), :]

        def body(i, total, k=k, r=r):
            at = pl.ds(pl.multiple_of(i * SUB, SUB), SUB)
            value = jnp.exp(t_ref[k, at, :] + (r + c_ref[at, :]))
            k_ref[k, at, :] = value
            return total + jnp.sum(value.reshape(SUB // 8, 8, LANES), axis=0)

        total = lax.fori_loop(0, c_ref.shape[0] // SUB, body, jnp.zeros((8, LANES), F32), unroll=2)
        rows_ref[pl.ds(step * tiles + k, 1), :] = jnp.sum(total, axis=0, keepdims=True)

    @pl.when(step == pl.num_programs(0) - 1)
    def _():
        rho_ref[...] = jnp.broadcast_to(rows_ref[...][None], rho_ref.shape)


def column_sum_kernel(ng, rho_ref, k_ref, sums_ref, u_ref, acc_ref):
    step = pl.program_id(0)
    tiles = k_ref.shape[0]

    @pl.when(step == 0)
    def _():
        u_ref[...] = ng / jnp.sum(rho_ref[...], axis=0)
        acc_ref[...] = jnp.zeros(acc_ref.shape, F32)

    u = [u_ref[pl.ds(step * tiles + k, 1), :] for k in range(tiles)]

    @pl.loop(0, acc_ref.shape[0], step=SUB)
    def _(c):
        at = pl.ds(pl.multiple_of(c, SUB), SUB)
        total = acc_ref[at, :]
        for k in range(tiles):
            total = total + k_ref[k, at, :] * u[k]
        acc_ref[at, :] = total

    @pl.when(step == pl.num_programs(0) - 1)
    def _():
        sums_ref[...] = jnp.broadcast_to(sum_to_rows(acc_ref[...])[None], sums_ref.shape)


def row_sum_kernel(np_, sums_ref, k_ref, v_ref, rho_ref, rows_ref):
    step = pl.program_id(0)
    tiles = k_ref.shape[0]

    @pl.when(step == 0)
    def _():
        to_columns(np_ / jnp.sum(sums_ref[...], axis=0), v_ref)

    def body(i, totals):
        at = pl.ds(pl.multiple_of(i * SUB, SUB), SUB)
        v = v_ref[at, :]
        return tuple(
            totals[k] + jnp.sum((k_ref[k, at, :] * v).reshape(SUB // 8, 8, LANES), axis=0)
            for k in range(tiles)
        )

    totals = lax.fori_loop(
        0, v_ref.shape[0] // SUB, body, tuple(jnp.zeros((8, LANES), F32) for _ in range(tiles))
    )
    for k in range(tiles):
        rows_ref[pl.ds(step * tiles + k, 1), :] = jnp.sum(totals[k], axis=0, keepdims=True)

    @pl.when(step == pl.num_programs(0) - 1)
    def _():
        rho_ref[...] = jnp.broadcast_to(rows_ref[...][None], rho_ref.shape)


def barycenter_kernel(ng, other, rho_ref, v_ref, k_ref, p_ref, out_ref, u_ref, mass_ref, w_ref):
    step = pl.program_id(0)
    tiles = k_ref.shape[0]
    cols, features = mass_ref.shape[0], out_ref.shape[1]
    core = lax.axis_index("core")
    begin = pl.multiple_of((1 - core if other else core) * cols, cols)

    @pl.when(step == 0)
    def _():
        u_ref[...] = ng / jnp.sum(rho_ref[...], axis=0)
        mass_ref[...] = jnp.zeros(mass_ref.shape, F32)
        out_ref[...] = jnp.zeros(out_ref.shape, F32)

    u = [u_ref[pl.ds(step * tiles + k, 1), :] for k in range(tiles)]

    @pl.loop(0, cols, step=SUB)
    def _(c):
        at = pl.ds(pl.multiple_of(c, SUB), SUB)
        source = pl.ds(pl.multiple_of(begin + c, SUB), SUB)
        v = v_ref[source, :]
        total = mass_ref[at, :]
        for k in range(tiles):
            w = k_ref[k, source, :] * u[k] * v
            total = total + w
            w_ref[at, k * LANES:(k + 1) * LANES] = w.astype(BF16)
        mass_ref[at, :] = total

    p = jnp.concatenate([p_ref[0, f] for f in range(p_ref.shape[1])], axis=1)
    out_ref[0:cols, :] += jnp.dot(w_ref[...], p, preferred_element_type=F32)

    @pl.when(step == pl.num_programs(0) - 1)
    def _():
        mass = jnp.sum(jnp.transpose(mass_ref[...]), axis=0, keepdims=True)
        out_ref[cols:, 0:cols] = jnp.broadcast_to(mass, (out_ref.shape[0] - cols, cols))


def mean_kernel(a_ref, b_ref, out_ref):
    owners = out_ref.shape[0]
    features = a_ref.shape[1]
    blocks = features // LANES
    rows = (out_ref.shape[1] - 16) // blocks
    cols = owners * rows
    mass = jnp.maximum(a_ref[cols:cols + 1, 0:cols] + b_ref[cols:cols + 1, 0:cols], 1e-30)
    log_mass = jnp.log(mass)
    inverse = jnp.transpose(jnp.broadcast_to(1.0 / mass, (LANES, cols)))
    for z in range(owners):
        at = slice(z * rows, (z + 1) * rows)
        for q in range(blocks):
            lanes = slice(q * LANES, (q + 1) * LANES)
            out_ref[z, q * rows:(q + 1) * rows, :] = (a_ref[at, lanes] + b_ref[at, lanes]) * inverse[at, :]
        part = jnp.concatenate([log_mass[:, at]] * (LANES // rows), axis=1)
        high = jnp.round(part * 16.0) * 0.0625
        low = part - high
        out_ref[z, blocks * rows:, :] = jnp.concatenate([high] * 8 + [low] * 8, axis=0)


def update_kernel(parts_ref, g_ref, n_ref, out_ref):
    sources = parts_ref.shape[0]
    rows = g_ref.shape[0]
    blocks = g_ref.shape[1] // LANES
    at = blocks * rows
    logs = jnp.concatenate(
        [parts_ref[d, at:at + 1, :] + parts_ref[d, at + 8:at + 9, :] for d in range(sources)], axis=0
    )
    weights = jnp.exp(logs - jnp.max(logs, axis=0, keepdims=True))
    weights = weights / jnp.sum(weights, axis=0, keepdims=True)
    columns = [
        jnp.transpose(jnp.broadcast_to(weights[d:d + 1, :], (LANES, LANES)))[0:rows, :]
        for d in range(sources)
    ]
    for q in range(blocks):
        lanes = slice(q * LANES, (q + 1) * LANES)
        total = parts_ref[0, q * rows:(q + 1) * rows, :] * columns[0]
        for d in range(1, sources):
            total = total + parts_ref[d, q * rows:(q + 1) * rows, :] * columns[d]
        out_ref[:, lanes] = g_ref[:, lanes].astype(F32) - total + n_ref[:, lanes]


def whole(shape):
    return pl.BlockSpec(shape, lambda b: (0,) * len(shape))


def permuted(a, axes, moved):
    sizes = [lax.axis_size(n) for n in axes]
    flat = lambda at: functools.reduce(lambda f, cn: f * cn[1] + cn[0] % cn[1], zip(at, sizes), 0)
    pairs = [(flat(at), flat(moved(*at))) for at in itertools.product(*map(range, sizes))]
    return lax.ppermute(a, axes, pairs)


def along(first, d, a):
    return permuted(
        a,
        ("x", "y", "core"),
        lambda x, y, c: (x + d, y, c) if (c == 0) == first else (x, y + d, c),
    )


def swap(a):
    return permuted(a, ("core",), lambda c: (1 - c,))


def gather_private(private):
    core = lax.axis_index("core")
    rows, width = private.shape
    halves = private.reshape(2, rows // 2, width)
    mine = lax.dynamic_index_in_dim(halves, core, 0, False)
    got = swap(lax.dynamic_index_in_dim(halves, 1 - core, 0, False))
    a0 = jnp.where(core == 0, jnp.stack([mine, got]), jnp.stack([got, mine]))
    a1 = along(True, 1, a0)
    a2 = along(True, -1, a0)
    a3 = along(True, 1, a1)
    s, t = jnp.stack([a0, a1]), jnp.stack([a2, a3])
    s1, s2 = along(False, 1, s), along(False, -1, s)
    t1, t2 = along(False, 1, t), along(False, -1, t)
    return s, t, s1, s2, t1, t2, along(False, 1, s1), along(False, -1, t2)


def gather_generated(generated):
    core = lax.axis_index("core")
    got = swap(generated)
    pair = jnp.where(core == 0, jnp.stack([generated, got]), jnp.stack([got, generated]))
    chain = [pair]
    for _ in range(4):
        chain.append(
            permuted(chain[-1], ("z", "core"), lambda z, c: (z + (1 if c == 0 else -1), c))
        )
    near = jnp.stack(chain[1:4])
    return pair, chain[4], near, swap(near)


def shards(private, generated, noise):
    rows_per, width = private.shape
    own, features = generated.shape
    nz, nx, ny = lax.axis_size("z"), lax.axis_size("x"), lax.axis_size("y")
    cols = own * nz * 2
    rows = rows_per // 2 * nx
    np_ = rows * nz * 2
    ng = cols * nx * ny
    scale = 2.0 / (features * EPS)
    row_tiles = rows // LANES
    col_tiles = cols // LANES
    tiles = 4
    steps = row_tiles // tiles
    block = tiles * LANES

    params = pltpu.CompilerParams(
        dimension_semantics=("arbitrary",), vmem_limit_bytes=40 * 1024 * 1024
    )
    p_shape = (nx, 2 * ny, rows_per // 2, width)
    p_spec = pl.BlockSpec((1,) + p_shape[1:], lambda b: (b, 0, 0, 0))
    t_spec = pl.BlockSpec((tiles, cols, LANES), lambda b: (b, 0, 0))
    t_shape = jax.ShapeDtypeStruct((row_tiles, cols, LANES), F32)
    row_shape = (nx * ny, row_tiles, LANES)
    col_shape = (nz * 2, col_tiles, LANES)
    row_out = jax.ShapeDtypeStruct(row_shape, F32)
    col_out = jax.ShapeDtypeStruct(col_shape, F32)
    rows_scratch = pltpu.VMEM((row_tiles, LANES), F32)
    cols_scratch = pltpu.VMEM((cols, LANES), F32)

    def over_rows(a):
        return lax.all_to_all(a, ("x", "y"), 0, 0, tiled=True)

    def over_columns(a):
        return lax.all_to_all(a, ("z", "core"), 0, 0, tiled=True)

    gathered = gather_private(private) + gather_generated(generated)
    p, t, lr = pl.pallas_call(
        functools.partial(score_kernel, scale),
        grid=(steps,),
        in_specs=[whole(a.shape) for a in gathered],
        out_specs=[whole(p_shape), t_spec, whole(row_shape)],
        out_shape=[jax.ShapeDtypeStruct(p_shape, BF16), t_shape, row_out],
        scratch_shapes=[pltpu.VMEM((cols, features), BF16), cols_scratch, rows_scratch],
        compiler_params=params,
        name="scores",
    )(*gathered)
    lr = over_rows(lr)

    r, lc = pl.pallas_call(
        functools.partial(first_column_kernel, math.log(ng)),
        grid=(steps,),
        in_specs=[whole(row_shape), t_spec],
        out_specs=[whole((row_tiles, LANES)), whole(col_shape)],
        out_shape=[jax.ShapeDtypeStruct((row_tiles, LANES), F32), col_out],
        scratch_shapes=[cols_scratch, cols_scratch],
        compiler_params=params,
        name="first_columns",
    )(lr, t)
    lc = over_columns(lc)

    k, rho = pl.pallas_call(
        functools.partial(plan_kernel, math.log(np_)),
        grid=(steps,),
        in_specs=[whole(col_shape), whole((row_tiles, LANES)), t_spec],
        out_specs=[t_spec, whole(row_shape)],
        out_shape=[t_shape, row_out],
        scratch_shapes=[cols_scratch, rows_scratch],
        compiler_params=params,
        name="plan",
    )(lc, r, t)
    rho = over_rows(rho)

    sums = pl.pallas_call(
        functools.partial(column_sum_kernel, float(ng)),
        grid=(steps,),
        in_specs=[whole(row_shape), t_spec],
        out_specs=whole(col_shape),
        out_shape=col_out,
        scratch_shapes=[rows_scratch, cols_scratch],
        compiler_params=params,
        name="column_sums",
    )(rho, k)
    sums = over_columns(sums)

    v, rho = pl.pallas_call(
        functools.partial(row_sum_kernel, float(np_)),
        grid=(steps,),
        in_specs=[whole(col_shape), t_spec],
        out_specs=[whole((cols, LANES)), whole(row_shape)],
        out_shape=[jax.ShapeDtypeStruct((cols, LANES), F32), row_out],
        scratch_shapes=[rows_scratch],
        compiler_params=params,
        name="row_sums",
    )(sums, k)
    rho = over_rows(rho)

    def barycenter(other):
        half = cols // 2
        return pl.pallas_call(
            functools.partial(barycenter_kernel, float(ng), other),
            grid=(steps,),
            in_specs=[whole(row_shape), whole((cols, LANES)), t_spec, p_spec],
            out_specs=whole((half + 8, features)),
            out_shape=jax.ShapeDtypeStruct((half + 8, features), F32),
            scratch_shapes=[
                rows_scratch,
                pltpu.VMEM((half, LANES), F32),
                pltpu.VMEM((half, block), BF16),
            ],
            compiler_params=params,
            cost_estimate=pl.CostEstimate(
                flops=2 * half * rows * features, bytes_accessed=16 << 20, transcendentals=0
            ),
            name="barycenter_other" if other else "barycenter_own",
        )(rho, v, k, p)

    theirs = swap(barycenter(True))
    mine = barycenter(False)
    small = pltpu.CompilerParams(vmem_limit_bytes=32 * 1024 * 1024)
    parts = pl.pallas_call(
        mean_kernel,
        out_shape=jax.ShapeDtypeStruct((nz, own * (features // LANES) + 16, LANES), F32),
        compiler_params=small,
        name="means",
    )(mine, theirs)
    parts = lax.all_to_all(parts.astype(F16), "z", 0, 0, tiled=True).astype(F32)

    return pl.pallas_call(
        update_kernel,
        out_shape=jax.ShapeDtypeStruct((own, features), F32),
        compiler_params=small,
        name="update",
    )(parts, generated, noise)


def solution(mesh):
    fine = Mesh(mesh.devices.reshape(8, 4, 4, 2), ("z", "x", "y", "core"))
    in_specs = (
        P(("z", "x"), ("y", "core")),
        P(("y", "core", "z", "x"), None),
        P(("y", "core", "z", "x"), None),
    )
    out_specs = P(("y", "core", "z", "x"), None)
    return jax.shard_map(shards, mesh=fine, in_specs=in_specs, out_specs=out_specs, check_vma=False)
```

```python
import functools
import itertools
import math

import jax
import jax.numpy as jnp
from jax import lax
from jax.experimental import pallas as pl
from jax.experimental.pallas import tpu as pltpu
from jax.sharding import Mesh
from jax.sharding import PartitionSpec as P


EPS = 0.02
F32 = jnp.float32
BF16 = jnp.bfloat16
F16 = jnp.float16
LANES = 128
SUB = 64


def to_rows(column):
    flat = jnp.transpose(column)[0:1, :]
    return jnp.concatenate(
        [flat[:, q * LANES:(q + 1) * LANES] for q in range(column.shape[0] // LANES)], axis=0
    )


def sum_to_rows(lanes):
    flat = jnp.sum(jnp.transpose(lanes), axis=0, keepdims=True)
    return jnp.concatenate(
        [flat[:, q * LANES:(q + 1) * LANES] for q in range(lanes.shape[0] // LANES)], axis=0
    )


def to_columns(rows, out_ref):
    for q in range(rows.shape[0]):
        out_ref[q * LANES:(q + 1) * LANES, :] = jnp.transpose(
            jnp.broadcast_to(rows[q:q + 1, :], (LANES, LANES))
        )


def logsumexp0(x):
    top = jnp.max(x, axis=0)
    return top + jnp.log2(jnp.sum(jnp.exp2(x - top[None]), axis=0))


def chunks(n):
    return [pl.ds(c, SUB) for c in range(0, n, SUB)]


def score_kernel(scale, *refs):
    blocks, (own_ref, far_ref, near_ref, swapped_ref) = refs[:8], refs[8:12]
    p_ref, t_ref, l_ref, g_ref, c0_ref, rows_ref = refs[12:]
    nx, slices, rows, width = p_ref.shape
    ny = slices // 2
    nz = 8
    x, y, z, core = (lax.axis_index(a) for a in ("x", "y", "z", "core"))

    first = ((0, -1), (1, -2))
    for ref, pair, second in zip(blocks, (0, 1, 0, 0, 1, 1, 0, 1), (0, 0, -1, 1, -1, 1, -2, 2)):
        for n in range(2):
            a, b = first[pair][n], second
            px = lax.rem(x + jnp.where(core == 0, a, b) + nx, nx)
            py = lax.rem(y + jnp.where(core == 0, b, a) + ny, ny)
            for f in range(2):
                p_ref[px, 2 * py + f] = ref[n, f]

    own = g_ref.shape[0] // (2 * nz)

    def put(ref, at, k):
        pz = lax.rem(z + k + nz, nz)
        for c in range(2):
            g = ref[at + (c,)]
            to = pl.ds(pl.multiple_of((c * nz + pz) * own, own), own)
            g_ref[to, :] = g
            g = g.astype(F32)
            sq = jnp.sum(g * g, axis=1, keepdims=True)
            c0_ref[to, :] = jnp.broadcast_to(sq * (-0.5 * scale), (own, LANES))

    sign = jnp.where(core == 0, -1, 1)
    put(own_ref, (), 0)
    put(far_ref, (), 4)
    for k in range(1, 4):
        put(near_ref, (k - 1,), sign * k)
        put(swapped_ref, (k - 1,), -sign * k)

    cols = g_ref.shape[0]
    wide = 2 * LANES

    def scores(n):
        at = pl.ds(n % (rows // wide) * wide, wide)
        p = jnp.concatenate([p_ref[n // (rows // wide), f, at, :] for f in range(slices)], axis=1)
        return lax.dot_general(g_ref[...], p, (((1,), (1,)), ((), ())), preferred_element_type=F32)

    def reduce(n):
        for k in (2 * n, 2 * n + 1):
            top = jnp.full((8, LANES), -jnp.inf, F32)
            for at in chunks(cols):
                top = jnp.maximum(top, jnp.max(t_ref[k, at, :].reshape(SUB // 8, 8, LANES), axis=0))
            top = jnp.max(top, axis=0, keepdims=True)
            total = jnp.zeros((8, LANES), F32)
            for at in chunks(cols):
                e = jnp.exp2(t_ref[k, at, :] - top)
                total = total + jnp.sum(e.reshape(SUB // 8, 8, LANES), axis=0)
            rows_ref[k:k + 1, :] = top + jnp.log2(jnp.sum(total, axis=0, keepdims=True))

    steps = nx * rows // wide
    for n in range(steps):
        cross = scores(n)
        if n:
            reduce(n - 1)
        for k in range(2):
            t_ref[2 * n + k] = cross[:, k * LANES:(k + 1) * LANES] * scale + c0_ref[...]
    reduce(steps - 1)
    l_ref[...] = jnp.broadcast_to(rows_ref[...][None], l_ref.shape)


def first_column_kernel(log_ng, l_ref, t_ref, g_ref, n_ref, r_ref, k_ref, lc_ref, base_ref, m_ref, s_ref):
    tiles, cols, _ = t_ref.shape
    base_ref[...] = g_ref[...].astype(F32) + n_ref[...]
    r_ref[...] = log_ng - logsumexp0(l_ref[...])
    r = [r_ref[n:n + 1, :] for n in range(tiles)]

    @pl.loop(0, cols, step=SUB)
    def _(c):
        at = pl.ds(pl.multiple_of(c, SUB), SUB)
        total = jnp.zeros((SUB, LANES), F32)
        for n in range(tiles):
            e = jnp.exp2(t_ref[n, at, :] + r[n])
            k_ref[n, at, :] = e
            total = total + e
        s_ref[at, :] = total

    sums = sum_to_rows(s_ref[...])
    lc_ref[...] = jnp.broadcast_to(jnp.log2(sums)[None], lc_ref.shape)

    @pl.when(jnp.min(sums) < 1e-30)
    def _():
        @pl.loop(0, cols, step=SUB)
        def _(c):
            at = pl.ds(pl.multiple_of(c, SUB), SUB)
            top = t_ref[0, at, :] + r[0]
            for n in range(1, tiles):
                top = jnp.maximum(top, t_ref[n, at, :] + r[n])
            total = jnp.zeros((SUB, LANES), F32)
            for n in range(tiles):
                total = total + jnp.exp2(t_ref[n, at, :] + r[n] - top)
            m_ref[at, :] = top
            s_ref[at, :] = total

        m = m_ref[...]
        top = jnp.max(m, axis=1, keepdims=True)
        total = jnp.sum(s_ref[...] * jnp.exp2(m - top), axis=1, keepdims=True)
        lc = to_rows(jnp.broadcast_to(top + jnp.log2(total), m.shape))
        lc_ref[...] = jnp.broadcast_to(lc[None], lc_ref.shape)


def scaled_row_sums(k_ref, v_ref, rho_ref):
    tiles, cols, _ = k_ref.shape

    def body(i, totals):
        at = pl.ds(pl.multiple_of(i * SUB, SUB), SUB)
        v = v_ref[at, :]
        return tuple(
            totals[n] + jnp.sum((k_ref[n, at, :] * v).reshape(SUB // 8, 8, LANES), axis=0)
            for n in range(tiles)
        )

    totals = lax.fori_loop(
        0, cols // SUB, body, tuple(jnp.zeros((8, LANES), F32) for _ in range(tiles))
    )
    rho = jnp.concatenate([jnp.sum(total, axis=0, keepdims=True) for total in totals], axis=0)
    rho_ref[...] = jnp.broadcast_to(rho[None], rho_ref.shape)


def second_row_kernel(log_np, lc_ref, r_ref, t_ref, old_ref, k_ref, rho_ref, v_ref):
    del old_ref
    tiles, cols, _ = t_ref.shape
    c1 = log_np - logsumexp0(lc_ref[...])
    fits = jnp.max(c1) <= 66.0
    to_columns(jnp.where(fits, jnp.exp2(c1), c1), v_ref)

    @pl.when(jnp.logical_not(fits))
    def _():
        @pl.loop(0, cols, step=SUB)
        def _(c):
            at = pl.ds(pl.multiple_of(c, SUB), SUB)
            for n in range(tiles):
                k_ref[n, at, :] = jnp.exp2(t_ref[n, at, :] + r_ref[n:n + 1, :] + v_ref[at, :])
            v_ref[at, :] = jnp.ones((SUB, LANES), F32)

    scaled_row_sums(k_ref, v_ref, rho_ref)


def column_sum_kernel(ng, rho_ref, k_ref, sums_ref, acc_ref):
    tiles, cols, _ = k_ref.shape
    scaled = ng / jnp.sum(rho_ref[...], axis=0)
    u = [scaled[n:n + 1, :] for n in range(tiles)]

    @pl.loop(0, cols, step=SUB)
    def _(c):
        at = pl.ds(pl.multiple_of(c, SUB), SUB)
        total = k_ref[0, at, :] * u[0]
        for n in range(1, tiles):
            total = total + k_ref[n, at, :] * u[n]
        acc_ref[at, :] = total

    sums_ref[...] = jnp.broadcast_to(sum_to_rows(acc_ref[...])[None], sums_ref.shape)


def row_sum_kernel(np_, sums_ref, k_ref, v_ref, rho_ref):
    to_columns(np_ / jnp.sum(sums_ref[...], axis=0), v_ref)
    scaled_row_sums(k_ref, v_ref, rho_ref)


def barycenter_kernel(ng, other, rho_ref, v_ref, k_ref, p_ref, out_ref, mass_ref, w_ref):
    tiles = k_ref.shape[0]
    cols = mass_ref.shape[0]
    core = lax.axis_index("core")
    begin = (1 - core if other else core) * cols
    scaled = ng / jnp.sum(rho_ref[...], axis=0)
    u = [scaled[n:n + 1, :] for n in range(tiles)]

    @pl.loop(0, cols, step=SUB)
    def _(c):
        at = pl.ds(pl.multiple_of(c, SUB), SUB)
        source = pl.ds(pl.multiple_of(begin + c, SUB), SUB)
        v = v_ref[source, :]
        total = jnp.zeros((SUB, LANES), F32)
        for n in range(tiles):
            w = k_ref[n, source, :] * u[n] * v
            total = total + w
            w_ref[at, n * LANES:(n + 1) * LANES] = w.astype(BF16)
        mass_ref[at, :] = total

    p = jnp.concatenate(
        [
            jnp.concatenate([p_ref[x, f] for f in range(p_ref.shape[1])], axis=1)
            for x in range(p_ref.shape[0])
        ],
        axis=0,
    )
    out_ref[0:cols, :] = jnp.dot(w_ref[...], p, preferred_element_type=F32)
    mass = jnp.sum(jnp.transpose(mass_ref[...]), axis=0, keepdims=True)
    out_ref[cols:, 0:cols] = jnp.broadcast_to(mass, (out_ref.shape[0] - cols, cols))


def mean_kernel(a_ref, b_ref, out_ref):
    owners = out_ref.shape[0]
    features = a_ref.shape[1]
    blocks = features // LANES
    rows = (out_ref.shape[1] - 16) // blocks
    cols = owners * rows
    mass = jnp.maximum(a_ref[cols:cols + 1, 0:cols] + b_ref[cols:cols + 1, 0:cols], 1e-30)
    log_mass = jnp.log2(mass)
    inverse = jnp.transpose(jnp.broadcast_to(1.0 / mass, (LANES, cols)))
    for z in range(owners):
        at = slice(z * rows, (z + 1) * rows)
        for q in range(blocks):
            lanes = slice(q * LANES, (q + 1) * LANES)
            out_ref[z, q * rows:(q + 1) * rows, :] = (a_ref[at, lanes] + b_ref[at, lanes]) * inverse[at, :]
        part = jnp.concatenate([log_mass[:, at]] * (LANES // rows), axis=1)
        high = jnp.round(part * 16.0) * 0.0625
        low = part - high
        out_ref[z, blocks * rows:, :] = jnp.concatenate([high] * 8 + [low] * 8, axis=0)


def update_kernel(parts_ref, base_ref, out_ref):
    sources = parts_ref.shape[0]
    rows = base_ref.shape[0]
    blocks = base_ref.shape[1] // LANES
    at = blocks * rows
    logs = jnp.concatenate(
        [parts_ref[d, at:at + 1, :] + parts_ref[d, at + 8:at + 9, :] for d in range(sources)], axis=0
    )
    weights = jnp.exp2(logs - jnp.max(logs, axis=0, keepdims=True))
    weights = weights / jnp.sum(weights, axis=0, keepdims=True)
    columns = [
        jnp.transpose(jnp.broadcast_to(weights[d:d + 1, :], (LANES, LANES)))[0:rows, :]
        for d in range(sources)
    ]
    for q in range(blocks):
        lanes = slice(q * LANES, (q + 1) * LANES)
        total = parts_ref[0, q * rows:(q + 1) * rows, :] * columns[0]
        for d in range(1, sources):
            total = total + parts_ref[d, q * rows:(q + 1) * rows, :] * columns[d]
        out_ref[:, lanes] = base_ref[:, lanes] - total


def permuted(a, axes, moved):
    sizes = [lax.axis_size(n) for n in axes]
    flat = lambda at: functools.reduce(lambda f, cn: f * cn[1] + cn[0] % cn[1], zip(at, sizes), 0)
    pairs = [(flat(at), flat(moved(*at))) for at in itertools.product(*map(range, sizes))]
    return lax.ppermute(a, axes, pairs)


def along(first, d, a):
    return permuted(
        a,
        ("x", "y", "core"),
        lambda x, y, c: (x + d, y, c) if (c == 0) == first else (x, y + d, c),
    )


def swap(a):
    return permuted(a, ("core",), lambda c: (1 - c,))


def gather_private(private):
    core = lax.axis_index("core")
    rows, width = private.shape
    halves = private.reshape(2, rows // 2, width)
    mine = lax.dynamic_index_in_dim(halves, core, 0, False)
    got = swap(lax.dynamic_index_in_dim(halves, 1 - core, 0, False))
    a0 = jnp.where(core == 0, jnp.stack([mine, got]), jnp.stack([got, mine]))
    a1 = along(True, 1, a0)
    a2 = along(True, -1, a0)
    a3 = along(True, 1, a1)
    s, t = jnp.stack([a0, a1]), jnp.stack([a2, a3])
    s1, s2 = along(False, 1, s), along(False, -1, s)
    t1, t2 = along(False, 1, t), along(False, -1, t)
    return s, t, s1, s2, t1, t2, along(False, 1, s1), along(False, -1, t2)


def gather_generated(generated):
    core = lax.axis_index("core")
    got = swap(generated)
    pair = jnp.where(core == 0, jnp.stack([generated, got]), jnp.stack([got, generated]))
    chain = [pair]
    for _ in range(4):
        chain.append(
            permuted(chain[-1], ("z", "core"), lambda z, c: (z + (1 if c == 0 else -1), c))
        )
    near = jnp.stack(chain[1:4])
    return pair, chain[4], near, swap(near)


def shards(private, generated, noise):
    rows_per, width = private.shape
    own, features = generated.shape
    nz, nx, ny = lax.axis_size("z"), lax.axis_size("x"), lax.axis_size("y")
    cols = own * nz * 2
    rows = rows_per // 2 * nx
    np_ = rows * nz * 2
    ng = cols * nx * ny
    scale = 2.0 / (features * EPS) * math.log2(math.e)
    row_tiles = rows // LANES
    col_tiles = cols // LANES
    half = cols // 2

    def call(body, name, out_shape, scratch, *args, limit=24, cost=None, aliases=None):
        return pl.pallas_call(
            body,
            out_shape=out_shape,
            scratch_shapes=scratch,
            compiler_params=pltpu.CompilerParams(vmem_limit_bytes=limit << 20),
            cost_estimate=cost,
            input_output_aliases=aliases or {},
            name=name,
        )(*args)

    def f32(*shape):
        return jax.ShapeDtypeStruct(shape, F32)

    row_out = f32(nx * ny, row_tiles, LANES)
    col_out = f32(nz * 2, col_tiles, LANES)
    k_shape = f32(row_tiles, cols, LANES)
    v_shape = f32(cols, LANES)
    lanes = pltpu.VMEM((cols, LANES), F32)

    def over_rows(a):
        return lax.all_to_all(a, ("x", "y"), 0, 0, tiled=True)

    def over_columns(a):
        return lax.all_to_all(a, ("z", "core"), 0, 0, tiled=True)

    gathered = gather_private(private) + gather_generated(generated)
    p, t, lr = call(
        functools.partial(score_kernel, scale),
        "scores",
        [jax.ShapeDtypeStruct((nx, 2 * ny, rows_per // 2, width), BF16), k_shape, row_out],
        [pltpu.VMEM((cols, features), BF16), lanes, pltpu.VMEM((row_tiles, LANES), F32)],
        *gathered,
    )
    r, k, lc, base = call(
        functools.partial(first_column_kernel, math.log2(ng)),
        "first_columns",
        [f32(row_tiles, LANES), k_shape, col_out, f32(own, features)],
        [lanes, lanes],
        over_rows(lr), t, generated, noise,
    )
    k, rho, v = call(
        functools.partial(second_row_kernel, math.log2(np_)),
        "second_rows",
        [k_shape, row_out, v_shape],
        [],
        over_columns(lc), r, t, k,
        aliases={3: 0},
    )
    sums = call(
        functools.partial(column_sum_kernel, float(ng)),
        "column_sums",
        col_out,
        [lanes],
        over_rows(rho), k,
    )
    v, rho = call(
        functools.partial(row_sum_kernel, float(np_)),
        "row_sums",
        [v_shape, row_out],
        [],
        over_columns(sums), k,
    )
    rho = over_rows(rho)

    def barycenter(other):
        return call(
            functools.partial(barycenter_kernel, float(ng), other),
            "barycenter_other" if other else "barycenter_own",
            f32(half + 8, features),
            [pltpu.VMEM((half, LANES), F32), pltpu.VMEM((half, rows), BF16)],
            rho, v, k, p,
            cost=pl.CostEstimate(
                flops=2 * half * rows * features, bytes_accessed=16 << 20, transcendentals=0
            ),
        )

    theirs = swap(barycenter(True))
    mine = barycenter(False)
    parts = call(
        mean_kernel, "means", f32(nz, own * (features // LANES) + 16, LANES), [], mine, theirs
    )
    parts = lax.all_to_all(parts.astype(F16), "z", 0, 0, tiled=True).astype(F32)
    return call(update_kernel, "update", f32(own, features), [], parts, base)


def solution(mesh):
    fine = Mesh(mesh.devices.reshape(8, 4, 4, 2), ("z", "x", "y", "core"))
    in_specs = (
        P(("z", "x"), ("y", "core")),
        P(("y", "core", "z", "x"), None),
        P(("y", "core", "z", "x"), None),
    )
    out_specs = P(("y", "core", "z", "x"), None)
    return jax.shard_map(shards, mesh=fine, in_specs=in_specs, out_specs=out_specs, check_vma=False)
```

```python
import functools
import itertools
import math

import jax
import jax.numpy as jnp
from jax import lax
from jax.experimental import pallas as pl
from jax.experimental.pallas import tpu as pltpu
from jax.sharding import Mesh
from jax.sharding import PartitionSpec as P


EPS = 0.02
F32 = jnp.float32
BF16 = jnp.bfloat16
F16 = jnp.float16
LANES = 128
SUB = 64


def to_rows(column):
    flat = jnp.transpose(column)[0:1, :]
    return jnp.concatenate(
        [flat[:, q * LANES:(q + 1) * LANES] for q in range(column.shape[0] // LANES)], axis=0
    )


def sum_to_rows(lanes):
    flat = jnp.sum(jnp.transpose(lanes), axis=0, keepdims=True)
    return jnp.concatenate(
        [flat[:, q * LANES:(q + 1) * LANES] for q in range(lanes.shape[0] // LANES)], axis=0
    )


def to_columns(rows, out_ref):
    for q in range(rows.shape[0]):
        out_ref[q * LANES:(q + 1) * LANES, :] = jnp.transpose(
            jnp.broadcast_to(rows[q:q + 1, :], (LANES, LANES))
        )


def logsumexp0(x):
    top = jnp.max(x, axis=0)
    return top + jnp.log2(jnp.sum(jnp.exp2(x - top[None]), axis=0))


def chunks(n):
    return [pl.ds(c, SUB) for c in range(0, n, SUB)]


WIDE = 2 * LANES


def place(ref, pair, second, p_ref):
    nx, ny = p_ref.shape[0], p_ref.shape[1] // 2
    x, y, core = (lax.axis_index(a) for a in ("x", "y", "core"))
    for n, first in enumerate(((0, -1), (1, -2))[pair]):
        px = lax.rem(x + jnp.where(core == 0, first, second) + nx, nx)
        py = lax.rem(y + jnp.where(core == 0, second, first) + ny, ny)
        for f in range(2):
            p_ref[px, 2 * py + f] = ref[n, f]


def score_columns(scale, blocks, p_ref, t_ref, g_ref, c0_ref, after):
    nx, slices, rows, _ = p_ref.shape
    nz = 8
    z = lax.axis_index("z")
    own = blocks[0][0].shape[1]
    starts = []
    for block, k in blocks:
        pz = lax.rem(z + k + nz, nz)
        for c in range(2):
            at = pl.ds(len(starts) * own, own)
            g = block[c]
            g_ref[at, :] = g
            g = g.astype(F32)
            sq = jnp.sum(g * g, axis=1, keepdims=True)
            c0_ref[at, :] = jnp.broadcast_to(sq * (-0.5 * scale), (own, LANES))
            starts.append(pl.multiple_of((c * nz + pz) * own, own))

    per = rows // WIDE
    for n in range(nx * per):
        at = pl.ds(n % per * WIDE, WIDE)
        p = jnp.concatenate([p_ref[n // per, f, at, :] for f in range(slices)], axis=1)
        cross = lax.dot_general(g_ref[...], p, (((1,), (1,)), ((), ())), preferred_element_type=F32)
        if n:
            after(n - 1)
        for k in range(2):
            for m, start in enumerate(starts):
                part = slice(m * own, (m + 1) * own)
                t_ref[2 * n + k, pl.ds(start, own), :] = (
                    cross[part, k * LANES:(k + 1) * LANES] * scale + c0_ref[part, :]
                )
    after(nx * per - 1)


def early_score_kernel(scale, *refs):
    blocks, (own_ref, far_ref, near_ref) = refs[:8], refs[8:11]
    p_ref, t_ref, g_ref, c0_ref = refs[11:]
    for ref, pair, second in zip(blocks, (0, 1, 0, 0, 1, 1, 0, 1), (0, 0, -1, 1, -1, 1, -2, 2)):
        place(ref, pair, second, p_ref)
    sign = jnp.where(lax.axis_index("core") == 0, -1, 1)
    columns = [(own_ref, 0), (far_ref, 4)] + [(near_ref.at[k - 1], sign * k) for k in (1, 2, 3)]
    score_columns(scale, columns, p_ref, t_ref, g_ref, c0_ref, lambda n: None)


def late_score_kernel(scale, swapped_ref, p_ref, old_ref, t_ref, l_ref, g_ref, c0_ref, rows_ref):
    del old_ref
    cols = t_ref.shape[1]

    def reduce(n):
        for k in (2 * n, 2 * n + 1):
            top = jnp.full((8, LANES), -jnp.inf, F32)
            for at in chunks(cols):
                top = jnp.maximum(top, jnp.max(t_ref[k, at, :].reshape(SUB // 8, 8, LANES), axis=0))
            top = jnp.max(top, axis=0, keepdims=True)
            total = jnp.zeros((8, LANES), F32)
            for at in chunks(cols):
                e = jnp.exp2(t_ref[k, at, :] - top)
                total = total + jnp.sum(e.reshape(SUB // 8, 8, LANES), axis=0)
            rows_ref[k:k + 1, :] = top + jnp.log2(jnp.sum(total, axis=0, keepdims=True))

    sign = jnp.where(lax.axis_index("core") == 0, 1, -1)
    columns = [(swapped_ref.at[k - 1], sign * k) for k in (1, 2, 3)]
    score_columns(scale, columns, p_ref, t_ref, g_ref, c0_ref, reduce)
    l_ref[...] = jnp.broadcast_to(rows_ref[...][None], l_ref.shape)


def first_column_kernel(log_ng, l_ref, t_ref, g_ref, n_ref, r_ref, k_ref, lc_ref, base_ref, m_ref, s_ref):
    tiles, cols, _ = t_ref.shape
    base_ref[...] = g_ref[...].astype(F32) + n_ref[...]
    r_ref[...] = log_ng - logsumexp0(l_ref[...])
    r = [r_ref[n:n + 1, :] for n in range(tiles)]

    @pl.loop(0, cols, step=SUB)
    def _(c):
        at = pl.ds(pl.multiple_of(c, SUB), SUB)
        total = jnp.zeros((SUB, LANES), F32)
        for n in range(tiles):
            e = jnp.exp2(t_ref[n, at, :] + r[n])
            k_ref[n, at, :] = e
            total = total + e
        s_ref[at, :] = total

    sums = sum_to_rows(s_ref[...])
    lc_ref[...] = jnp.broadcast_to(jnp.log2(sums)[None], lc_ref.shape)

    @pl.when(jnp.min(sums) < 1e-30)
    def _():
        @pl.loop(0, cols, step=SUB)
        def _(c):
            at = pl.ds(pl.multiple_of(c, SUB), SUB)
            top = t_ref[0, at, :] + r[0]
            for n in range(1, tiles):
                top = jnp.maximum(top, t_ref[n, at, :] + r[n])
            total = jnp.zeros((SUB, LANES), F32)
            for n in range(tiles):
                total = total + jnp.exp2(t_ref[n, at, :] + r[n] - top)
            m_ref[at, :] = top
            s_ref[at, :] = total

        m = m_ref[...]
        top = jnp.max(m, axis=1, keepdims=True)
        total = jnp.sum(s_ref[...] * jnp.exp2(m - top), axis=1, keepdims=True)
        lc = to_rows(jnp.broadcast_to(top + jnp.log2(total), m.shape))
        lc_ref[...] = jnp.broadcast_to(lc[None], lc_ref.shape)


def scaled_row_sums(k_ref, v_ref, rho_ref):
    tiles, cols, _ = k_ref.shape

    def body(i, totals):
        at = pl.ds(pl.multiple_of(i * SUB, SUB), SUB)
        v = v_ref[at, :]
        return tuple(
            totals[n] + jnp.sum((k_ref[n, at, :] * v).reshape(SUB // 8, 8, LANES), axis=0)
            for n in range(tiles)
        )

    totals = lax.fori_loop(
        0, cols // SUB, body, tuple(jnp.zeros((8, LANES), F32) for _ in range(tiles))
    )
    rho = jnp.concatenate([jnp.sum(total, axis=0, keepdims=True) for total in totals], axis=0)
    rho_ref[...] = jnp.broadcast_to(rho[None], rho_ref.shape)


def second_row_kernel(log_np, lc_ref, r_ref, t_ref, old_ref, k_ref, rho_ref, v_ref):
    del old_ref
    tiles, cols, _ = t_ref.shape
    c1 = log_np - logsumexp0(lc_ref[...])
    fits = jnp.max(c1) <= 66.0
    to_columns(jnp.where(fits, jnp.exp2(c1), c1), v_ref)

    @pl.when(jnp.logical_not(fits))
    def _():
        @pl.loop(0, cols, step=SUB)
        def _(c):
            at = pl.ds(pl.multiple_of(c, SUB), SUB)
            for n in range(tiles):
                k_ref[n, at, :] = jnp.exp2(t_ref[n, at, :] + r_ref[n:n + 1, :] + v_ref[at, :])
            v_ref[at, :] = jnp.ones((SUB, LANES), F32)

    scaled_row_sums(k_ref, v_ref, rho_ref)


def column_sum_kernel(ng, rho_ref, k_ref, sums_ref, acc_ref):
    tiles, cols, _ = k_ref.shape
    scaled = ng / jnp.sum(rho_ref[...], axis=0)
    u = [scaled[n:n + 1, :] for n in range(tiles)]

    @pl.loop(0, cols, step=SUB)
    def _(c):
        at = pl.ds(pl.multiple_of(c, SUB), SUB)
        total = k_ref[0, at, :] * u[0]
        for n in range(1, tiles):
            total = total + k_ref[n, at, :] * u[n]
        acc_ref[at, :] = total

    sums_ref[...] = jnp.broadcast_to(sum_to_rows(acc_ref[...])[None], sums_ref.shape)


def row_sum_kernel(np_, sums_ref, k_ref, v_ref, rho_ref):
    to_columns(np_ / jnp.sum(sums_ref[...], axis=0), v_ref)
    scaled_row_sums(k_ref, v_ref, rho_ref)


def barycenter_kernel(ng, other, rho_ref, v_ref, k_ref, p_ref, out_ref, mass_ref, w_ref):
    tiles = k_ref.shape[0]
    cols = mass_ref.shape[0]
    core = lax.axis_index("core")
    begin = (1 - core if other else core) * cols
    scaled = ng / jnp.sum(rho_ref[...], axis=0)
    u = [scaled[n:n + 1, :] for n in range(tiles)]

    @pl.loop(0, cols, step=SUB)
    def _(c):
        at = pl.ds(pl.multiple_of(c, SUB), SUB)
        source = pl.ds(pl.multiple_of(begin + c, SUB), SUB)
        v = v_ref[source, :]
        total = jnp.zeros((SUB, LANES), F32)
        for n in range(tiles):
            w = k_ref[n, source, :] * u[n] * v
            total = total + w
            w_ref[at, n * LANES:(n + 1) * LANES] = w.astype(BF16)
        mass_ref[at, :] = total

    p = jnp.concatenate(
        [
            jnp.concatenate([p_ref[x, f] for f in range(p_ref.shape[1])], axis=1)
            for x in range(p_ref.shape[0])
        ],
        axis=0,
    )
    out_ref[0:cols, :] = jnp.dot(w_ref[...], p, preferred_element_type=F32)
    mass = jnp.sum(jnp.transpose(mass_ref[...]), axis=0, keepdims=True)
    out_ref[cols:, 0:cols] = jnp.broadcast_to(mass, (out_ref.shape[0] - cols, cols))


def mean_kernel(a_ref, b_ref, out_ref):
    owners = out_ref.shape[0]
    features = a_ref.shape[1]
    blocks = features // LANES
    rows = (out_ref.shape[1] - 16) // blocks
    cols = owners * rows
    mass = jnp.maximum(a_ref[cols:cols + 1, 0:cols] + b_ref[cols:cols + 1, 0:cols], 1e-30)
    log_mass = jnp.log2(mass)
    inverse = jnp.transpose(jnp.broadcast_to(1.0 / mass, (LANES, cols)))
    for z in range(owners):
        at = slice(z * rows, (z + 1) * rows)
        for q in range(blocks):
            lanes = slice(q * LANES, (q + 1) * LANES)
            out_ref[z, q * rows:(q + 1) * rows, :] = (a_ref[at, lanes] + b_ref[at, lanes]) * inverse[at, :]
        part = jnp.concatenate([log_mass[:, at]] * (LANES // rows), axis=1)
        high = jnp.round(part * 16.0) * 0.0625
        low = part - high
        out_ref[z, blocks * rows:, :] = jnp.concatenate([high] * 8 + [low] * 8, axis=0)


def update_kernel(parts_ref, base_ref, out_ref):
    sources = parts_ref.shape[0]
    rows = base_ref.shape[0]
    blocks = base_ref.shape[1] // LANES
    at = blocks * rows
    logs = jnp.concatenate(
        [parts_ref[d, at:at + 1, :] + parts_ref[d, at + 8:at + 9, :] for d in range(sources)], axis=0
    )
    weights = jnp.exp2(logs - jnp.max(logs, axis=0, keepdims=True))
    weights = weights / jnp.sum(weights, axis=0, keepdims=True)
    columns = [
        jnp.transpose(jnp.broadcast_to(weights[d:d + 1, :], (LANES, LANES)))[0:rows, :]
        for d in range(sources)
    ]
    for q in range(blocks):
        lanes = slice(q * LANES, (q + 1) * LANES)
        total = parts_ref[0, q * rows:(q + 1) * rows, :] * columns[0]
        for d in range(1, sources):
            total = total + parts_ref[d, q * rows:(q + 1) * rows, :] * columns[d]
        out_ref[:, lanes] = base_ref[:, lanes] - total


def permuted(a, axes, moved):
    sizes = [lax.axis_size(n) for n in axes]
    flat = lambda at: functools.reduce(lambda f, cn: f * cn[1] + cn[0] % cn[1], zip(at, sizes), 0)
    pairs = [(flat(at), flat(moved(*at))) for at in itertools.product(*map(range, sizes))]
    return lax.ppermute(a, axes, pairs)


def along(first, d, a):
    return permuted(
        a,
        ("x", "y", "core"),
        lambda x, y, c: (x + d, y, c) if (c == 0) == first else (x, y + d, c),
    )


def swap(a):
    return permuted(a, ("core",), lambda c: (1 - c,))


def gather(private, generated):
    core = lax.axis_index("core")
    rows, width = private.shape
    mine, got = private.reshape(2, rows // 2, width), swap(private).reshape(2, rows // 2, width)
    a0 = jnp.where(core == 0, jnp.stack([mine[0], got[0]]), jnp.stack([got[1], mine[1]]))
    a1, a2 = along(True, 1, a0), along(True, -1, a0)
    a3 = along(True, 2, a0)
    s, t = jnp.stack([a0, a1]), jnp.stack([a2, a3])
    s1, t2, t1, s2 = along(False, 1, s), along(False, -1, t), along(False, 1, t), along(False, -1, s)
    h1, h2 = along(False, 1, s1), along(False, -1, t2)

    got = swap(generated)
    chain = [jnp.where(core == 0, jnp.stack([generated, got]), jnp.stack([got, generated]))]
    for _ in range(4):
        chain.append(
            permuted(chain[-1], ("z", "core"), lambda z, c: (z + (1 if c == 0 else -1), c))
        )
    near = jnp.stack(chain[1:4])
    near, far, t1, s2, h1, h2 = lax.optimization_barrier((near, chain[4], t1, s2, h1, h2))
    return (s, t, s1, s2, t1, t2, h1, h2), (chain[0], far, near), swap(near)


def shards(private, generated, noise):
    rows_per, width = private.shape
    own, features = generated.shape
    nz, nx, ny = lax.axis_size("z"), lax.axis_size("x"), lax.axis_size("y")
    cols = own * nz * 2
    rows = rows_per // 2 * nx
    np_ = rows * nz * 2
    ng = cols * nx * ny
    scale = 2.0 / (features * EPS) * math.log2(math.e)
    row_tiles = rows // LANES
    col_tiles = cols // LANES
    half = cols // 2

    def call(body, name, out_shape, scratch, *args, limit=24, cost=None, aliases=None):
        return pl.pallas_call(
            body,
            out_shape=out_shape,
            scratch_shapes=scratch,
            compiler_params=pltpu.CompilerParams(vmem_limit_bytes=limit << 20),
            cost_estimate=cost,
            input_output_aliases=aliases or {},
            name=name,
        )(*args)

    def f32(*shape):
        return jax.ShapeDtypeStruct(shape, F32)

    row_out = f32(nx * ny, row_tiles, LANES)
    col_out = f32(nz * 2, col_tiles, LANES)
    k_shape = f32(row_tiles, cols, LANES)
    v_shape = f32(cols, LANES)
    lanes = pltpu.VMEM((cols, LANES), F32)

    def over_rows(a):
        return lax.all_to_all(a, ("x", "y"), 0, 0, tiled=True)

    def over_columns(a):
        return lax.all_to_all(a, ("z", "core"), 0, 0, tiled=True)

    blocks, columns, swapped = gather(private, generated)
    others = cols * 3 // 8
    p, t = call(
        functools.partial(early_score_kernel, scale),
        "early_scores",
        [jax.ShapeDtypeStruct((nx, 2 * ny, rows_per // 2, width), BF16), k_shape],
        [pltpu.VMEM((cols - others, features), BF16), pltpu.VMEM((cols - others, LANES), F32)],
        *blocks, *columns,
        cost=pl.CostEstimate(
            flops=2 * (cols - others) * rows * features, bytes_accessed=24 << 20, transcendentals=0
        ),
    )
    t, lr = call(
        functools.partial(late_score_kernel, scale),
        "late_scores",
        [k_shape, row_out],
        [
            pltpu.VMEM((others, features), BF16),
            pltpu.VMEM((others, LANES), F32),
            pltpu.VMEM((row_tiles, LANES), F32),
        ],
        swapped, p, t,
        aliases={2: 0},
    )
    r, k, lc, base = call(
        functools.partial(first_column_kernel, math.log2(ng)),
        "first_columns",
        [f32(row_tiles, LANES), k_shape, col_out, f32(own, features)],
        [lanes, lanes],
        over_rows(lr), t, generated, noise,
    )
    k, rho, v = call(
        functools.partial(second_row_kernel, math.log2(np_)),
        "second_rows",
        [k_shape, row_out, v_shape],
        [],
        over_columns(lc), r, t, k,
        aliases={3: 0},
    )
    sums = call(
        functools.partial(column_sum_kernel, float(ng)),
        "column_sums",
        col_out,
        [lanes],
        over_rows(rho), k,
    )
    v, rho = call(
        functools.partial(row_sum_kernel, float(np_)),
        "row_sums",
        [v_shape, row_out],
        [],
        over_columns(sums), k,
    )
    rho = over_rows(rho)

    def barycenter(other):
        return call(
            functools.partial(barycenter_kernel, float(ng), other),
            "barycenter_other" if other else "barycenter_own",
            f32(half + 8, features),
            [pltpu.VMEM((half, LANES), F32), pltpu.VMEM((half, rows), BF16)],
            rho, v, k, p,
            cost=pl.CostEstimate(
                flops=2 * half * rows * features, bytes_accessed=16 << 20, transcendentals=0
            ),
        )

    theirs = swap(barycenter(True))
    mine = barycenter(False)
    parts = call(
        mean_kernel, "means", f32(nz, own * (features // LANES) + 16, LANES), [], mine, theirs
    )
    parts = lax.all_to_all(parts.astype(F16), "z", 0, 0, tiled=True).astype(F32)
    return call(update_kernel, "update", f32(own, features), [], parts, base)


def solution(mesh):
    fine = Mesh(mesh.devices.reshape(8, 4, 4, 2), ("z", "x", "y", "core"))
    in_specs = (
        P(("z", "x"), ("y", "core")),
        P(("y", "core", "z", "x"), None),
        P(("y", "core", "z", "x"), None),
    )
    out_specs = P(("y", "core", "z", "x"), None)
    return jax.shard_map(shards, mesh=fine, in_specs=in_specs, out_specs=out_specs, check_vma=False)
```

```python
import functools
import itertools
import math

import jax
import jax.numpy as jnp
from jax import lax
from jax.experimental import pallas as pl
from jax.experimental.pallas import tpu as pltpu
from jax.sharding import Mesh
from jax.sharding import PartitionSpec as P


EPS = 0.02
F32 = jnp.float32
BF16 = jnp.bfloat16
F16 = jnp.float16
LANES = 128
SUB = 64


def to_rows(column):
    flat = jnp.transpose(column)[0:1, :]
    return jnp.concatenate(
        [flat[:, q * LANES:(q + 1) * LANES] for q in range(column.shape[0] // LANES)], axis=0
    )


def sum_to_rows(lanes):
    flat = jnp.sum(jnp.transpose(lanes), axis=0, keepdims=True)
    return jnp.concatenate(
        [flat[:, q * LANES:(q + 1) * LANES] for q in range(lanes.shape[0] // LANES)], axis=0
    )


def to_columns(rows, out_ref):
    for q in range(rows.shape[0]):
        out_ref[q * LANES:(q + 1) * LANES, :] = jnp.transpose(
            jnp.broadcast_to(rows[q:q + 1, :], (LANES, LANES))
        )


def logsumexp0(x):
    top = jnp.max(x, axis=0)
    return top + jnp.log2(jnp.sum(jnp.exp2(x - top[None]), axis=0))


def chunks(n):
    return [pl.ds(c, SUB) for c in range(0, n, SUB)]


WIDE = 2 * LANES


def place(ref, pair, second, p_ref):
    nx, ny = p_ref.shape[0], p_ref.shape[1] // 2
    x, y, core = (lax.axis_index(a) for a in ("x", "y", "core"))
    for n, first in enumerate(((0, -1), (1, -2))[pair]):
        px = lax.rem(x + jnp.where(core == 0, first, second) + nx, nx)
        py = lax.rem(y + jnp.where(core == 0, second, first) + ny, ny)
        for f in range(2):
            p_ref[px, 2 * py + f] = ref[n, f]


def score_columns(scale, blocks, p_ref, t_ref, rows_ref, g_ref, c0_ref):
    nx, slices, rows, _ = p_ref.shape
    nz = 8
    z = lax.axis_index("z")
    own = blocks[0][0].shape[1]
    starts = []
    for block, k in blocks:
        pz = lax.rem(z + k + nz, nz)
        for c in range(2):
            at = pl.ds(len(starts) * own, own)
            g = block[c]
            g_ref[at, :] = g
            g = g.astype(F32)
            sq = jnp.sum(g * g, axis=1, keepdims=True)
            c0_ref[at, :] = jnp.broadcast_to(sq * (-0.5 * scale), (own, LANES))
            starts.append(pl.multiple_of((c * nz + pz) * own, own))

    def reduce(k):
        top = jnp.full((8, LANES), -jnp.inf, F32)
        for start in starts:
            t = t_ref[k, pl.ds(start, own), :]
            top = jnp.maximum(top, jnp.max(t.reshape(own // 8, 8, LANES), axis=0))
        top = jnp.max(top, axis=0, keepdims=True)
        total = jnp.zeros((8, LANES), F32)
        for start in starts:
            e = jnp.exp2(t_ref[k, pl.ds(start, own), :] - top)
            total = total + jnp.sum(e.reshape(own // 8, 8, LANES), axis=0)
        rows_ref[k:k + 1, :] = top + jnp.log2(jnp.sum(total, axis=0, keepdims=True))

    per = rows // WIDE
    for n in range(nx * per):
        at = pl.ds(n % per * WIDE, WIDE)
        p = jnp.concatenate([p_ref[n // per, f, at, :] for f in range(slices)], axis=1)
        cross = lax.dot_general(g_ref[...], p, (((1,), (1,)), ((), ())), preferred_element_type=F32)
        if n:
            reduce(2 * n - 2)
            reduce(2 * n - 1)
        for k in range(2):
            for m, start in enumerate(starts):
                part = slice(m * own, (m + 1) * own)
                t_ref[2 * n + k, pl.ds(start, own), :] = (
                    cross[part, k * LANES:(k + 1) * LANES] * scale + c0_ref[part, :]
                )
    reduce(2 * nx * per - 2)
    reduce(2 * nx * per - 1)


def early_score_kernel(scale, *refs):
    blocks, (own_ref, far_ref, near_ref) = refs[:8], refs[8:11]
    p_ref, t_ref, rows_ref, g_ref, c0_ref = refs[11:]
    for ref, pair, second in zip(blocks, (0, 1, 0, 0, 1, 1, 0, 1), (0, 0, -1, 1, -1, 1, -2, 2)):
        place(ref, pair, second, p_ref)
    sign = jnp.where(lax.axis_index("core") == 0, -1, 1)
    columns = [(own_ref, 0), (far_ref, 4)] + [(near_ref.at[k - 1], sign * k) for k in (1, 2, 3)]
    score_columns(scale, columns, p_ref, t_ref, rows_ref, g_ref, c0_ref)


def late_score_kernel(scale, swapped_ref, p_ref, early_ref, old_ref, t_ref, l_ref, g_ref, c0_ref, rows_ref):
    del old_ref
    sign = jnp.where(lax.axis_index("core") == 0, 1, -1)
    columns = [(swapped_ref.at[k - 1], sign * k) for k in (1, 2, 3)]
    score_columns(scale, columns, p_ref, t_ref, rows_ref, g_ref, c0_ref)
    late, early = rows_ref[...], early_ref[...]
    top = jnp.maximum(late, early)
    total = top + jnp.log2(jnp.exp2(late - top) + jnp.exp2(early - top))
    l_ref[...] = jnp.broadcast_to(total[None], l_ref.shape)


def first_column_kernel(log_ng, l_ref, t_ref, g_ref, n_ref, r_ref, k_ref, lc_ref, base_ref, m_ref, s_ref):
    tiles, cols, _ = t_ref.shape
    base_ref[...] = g_ref[...].astype(F32) + n_ref[...]
    r_ref[...] = log_ng - logsumexp0(l_ref[...])
    r = [r_ref[n:n + 1, :] for n in range(tiles)]

    @pl.loop(0, cols, step=SUB)
    def _(c):
        at = pl.ds(pl.multiple_of(c, SUB), SUB)
        total = jnp.zeros((SUB, LANES), F32)
        for n in range(tiles):
            e = jnp.exp2(t_ref[n, at, :] + r[n])
            k_ref[n, at, :] = e
            total = total + e
        s_ref[at, :] = total

    sums = sum_to_rows(s_ref[...])
    lc_ref[...] = jnp.broadcast_to(jnp.log2(sums)[None], lc_ref.shape)

    @pl.when(jnp.min(sums) < 1e-30)
    def _():
        @pl.loop(0, cols, step=SUB)
        def _(c):
            at = pl.ds(pl.multiple_of(c, SUB), SUB)
            top = t_ref[0, at, :] + r[0]
            for n in range(1, tiles):
                top = jnp.maximum(top, t_ref[n, at, :] + r[n])
            total = jnp.zeros((SUB, LANES), F32)
            for n in range(tiles):
                total = total + jnp.exp2(t_ref[n, at, :] + r[n] - top)
            m_ref[at, :] = top
            s_ref[at, :] = total

        m = m_ref[...]
        top = jnp.max(m, axis=1, keepdims=True)
        total = jnp.sum(s_ref[...] * jnp.exp2(m - top), axis=1, keepdims=True)
        lc = to_rows(jnp.broadcast_to(top + jnp.log2(total), m.shape))
        lc_ref[...] = jnp.broadcast_to(lc[None], lc_ref.shape)


def scaled_row_sums(k_ref, v_ref, rho_ref):
    tiles, cols, _ = k_ref.shape

    def body(i, totals):
        at = pl.ds(pl.multiple_of(i * SUB, SUB), SUB)
        v = v_ref[at, :]
        return tuple(
            totals[n] + jnp.sum((k_ref[n, at, :] * v).reshape(SUB // 8, 8, LANES), axis=0)
            for n in range(tiles)
        )

    totals = lax.fori_loop(
        0, cols // SUB, body, tuple(jnp.zeros((8, LANES), F32) for _ in range(tiles))
    )
    rho = jnp.concatenate([jnp.sum(total, axis=0, keepdims=True) for total in totals], axis=0)
    rho_ref[...] = jnp.broadcast_to(rho[None], rho_ref.shape)


def second_row_kernel(log_np, lc_ref, r_ref, t_ref, old_ref, k_ref, rho_ref, v_ref):
    del old_ref
    tiles, cols, _ = t_ref.shape
    c1 = log_np - logsumexp0(lc_ref[...])
    fits = jnp.max(c1) <= 66.0
    to_columns(jnp.where(fits, jnp.exp2(c1), c1), v_ref)

    @pl.when(jnp.logical_not(fits))
    def _():
        @pl.loop(0, cols, step=SUB)
        def _(c):
            at = pl.ds(pl.multiple_of(c, SUB), SUB)
            for n in range(tiles):
                k_ref[n, at, :] = jnp.exp2(t_ref[n, at, :] + r_ref[n:n + 1, :] + v_ref[at, :])
            v_ref[at, :] = jnp.ones((SUB, LANES), F32)

    scaled_row_sums(k_ref, v_ref, rho_ref)


def column_sum_kernel(ng, rho_ref, k_ref, sums_ref, acc_ref):
    tiles, cols, _ = k_ref.shape
    scaled = ng / jnp.sum(rho_ref[...], axis=0)
    u = [scaled[n:n + 1, :] for n in range(tiles)]

    @pl.loop(0, cols, step=SUB)
    def _(c):
        at = pl.ds(pl.multiple_of(c, SUB), SUB)
        total = k_ref[0, at, :] * u[0]
        for n in range(1, tiles):
            total = total + k_ref[n, at, :] * u[n]
        acc_ref[at, :] = total

    sums_ref[...] = jnp.broadcast_to(sum_to_rows(acc_ref[...])[None], sums_ref.shape)


def row_sum_kernel(np_, sums_ref, k_ref, v_ref, rho_ref):
    to_columns(np_ / jnp.sum(sums_ref[...], axis=0), v_ref)
    scaled_row_sums(k_ref, v_ref, rho_ref)


def barycenter_kernel(ng, other, rho_ref, v_ref, k_ref, p_ref, out_ref, mass_ref, w_ref):
    tiles = k_ref.shape[0]
    cols = mass_ref.shape[0]
    core = lax.axis_index("core")
    begin = (1 - core if other else core) * cols
    scaled = ng / jnp.sum(rho_ref[...], axis=0)
    u = [scaled[n:n + 1, :] for n in range(tiles)]

    p = jnp.concatenate(
        [
            jnp.concatenate([p_ref[x, f] for f in range(p_ref.shape[1])], axis=1)
            for x in range(p_ref.shape[0])
        ],
        axis=0,
    )
    part = cols // 2
    for first in range(0, cols, part):
        for c in range(first, first + part, SUB):
            at = pl.ds(c, SUB)
            source = pl.ds(pl.multiple_of(begin + c, SUB), SUB)
            v = v_ref[source, :]
            total = jnp.zeros((SUB, LANES), F32)
            for n in range(tiles):
                w = k_ref[n, source, :] * u[n] * v
                total = total + w
                w_ref[at, n * LANES:(n + 1) * LANES] = w.astype(BF16)
            mass_ref[at, :] = total
        out_ref[first:first + part, :] = jnp.dot(
            w_ref[first:first + part, :], p, preferred_element_type=F32
        )
    mass = jnp.sum(jnp.transpose(mass_ref[...]), axis=0, keepdims=True)
    out_ref[cols:, 0:cols] = jnp.broadcast_to(mass, (out_ref.shape[0] - cols, cols))


def mean_kernel(a_ref, b_ref, out_ref):
    owners = out_ref.shape[0]
    features = a_ref.shape[1]
    blocks = features // LANES
    rows = (out_ref.shape[1] - 16) // blocks
    cols = owners * rows
    mass = jnp.maximum(a_ref[cols:cols + 1, 0:cols] + b_ref[cols:cols + 1, 0:cols], 1e-30)
    log_mass = jnp.log2(mass)
    inverse = jnp.transpose(jnp.broadcast_to(1.0 / mass, (LANES, cols)))
    for z in range(owners):
        at = slice(z * rows, (z + 1) * rows)
        for q in range(blocks):
            lanes = slice(q * LANES, (q + 1) * LANES)
            out_ref[z, q * rows:(q + 1) * rows, :] = (a_ref[at, lanes] + b_ref[at, lanes]) * inverse[at, :]
        part = jnp.concatenate([log_mass[:, at]] * (LANES // rows), axis=1)
        high = jnp.round(part * 16.0) * 0.0625
        low = part - high
        out_ref[z, blocks * rows:, :] = jnp.concatenate([high] * 8 + [low] * 8, axis=0)


def update_kernel(parts_ref, base_ref, out_ref):
    sources = parts_ref.shape[0]
    rows = base_ref.shape[0]
    blocks = base_ref.shape[1] // LANES
    at = blocks * rows
    logs = jnp.concatenate(
        [parts_ref[d, at:at + 1, :] + parts_ref[d, at + 8:at + 9, :] for d in range(sources)], axis=0
    )
    weights = jnp.exp2(logs - jnp.max(logs, axis=0, keepdims=True))
    weights = weights / jnp.sum(weights, axis=0, keepdims=True)
    columns = [
        jnp.transpose(jnp.broadcast_to(weights[d:d + 1, :], (LANES, LANES)))[0:rows, :]
        for d in range(sources)
    ]
    for q in range(blocks):
        lanes = slice(q * LANES, (q + 1) * LANES)
        total = parts_ref[0, q * rows:(q + 1) * rows, :] * columns[0]
        for d in range(1, sources):
            total = total + parts_ref[d, q * rows:(q + 1) * rows, :] * columns[d]
        out_ref[:, lanes] = base_ref[:, lanes] - total


def permuted(a, axes, moved):
    sizes = [lax.axis_size(n) for n in axes]
    flat = lambda at: functools.reduce(lambda f, cn: f * cn[1] + cn[0] % cn[1], zip(at, sizes), 0)
    pairs = [(flat(at), flat(moved(*at))) for at in itertools.product(*map(range, sizes))]
    return lax.ppermute(a, axes, pairs)


def along(first, d, a):
    return permuted(
        a,
        ("x", "y", "core"),
        lambda x, y, c: (x + d, y, c) if (c == 0) == first else (x, y + d, c),
    )


def swap(a):
    return permuted(a, ("core",), lambda c: (1 - c,))


def gather(private, generated):
    core = lax.axis_index("core")
    rows, width = private.shape
    mine, got = private.reshape(2, rows // 2, width), swap(private).reshape(2, rows // 2, width)
    a0 = jnp.where(core == 0, jnp.stack([mine[0], got[0]]), jnp.stack([got[1], mine[1]]))
    a1, a2 = along(True, 1, a0), along(True, -1, a0)
    a3 = along(True, 2, a0)
    s, t = jnp.stack([a0, a1]), jnp.stack([a2, a3])
    s1, t2, t1, s2 = along(False, 1, s), along(False, -1, t), along(False, 1, t), along(False, -1, s)
    h1, h2 = along(False, 1, s1), along(False, -1, t2)

    got = swap(generated)
    g0 = jnp.where(core == 0, jnp.stack([generated, got]), jnp.stack([got, generated]))

    def onward(g, d):
        return permuted(g, ("z", "core"), lambda z, c: (z + (d if c == 0 else -d), c))

    g1, g2 = onward(g0, 1), onward(g0, 2)
    g34 = onward(jnp.stack([g1, g2]), 2)
    near, far = jnp.stack([g1, g2, g34[0]]), g34[1]
    near, far, t1, s2, h1, h2 = lax.optimization_barrier((near, far, t1, s2, h1, h2))
    return (s, t, s1, s2, t1, t2, h1, h2), (g0, far, near), swap(near)


def shards(private, generated, noise):
    rows_per, width = private.shape
    own, features = generated.shape
    nz, nx, ny = lax.axis_size("z"), lax.axis_size("x"), lax.axis_size("y")
    cols = own * nz * 2
    rows = rows_per // 2 * nx
    np_ = rows * nz * 2
    ng = cols * nx * ny
    scale = 2.0 / (features * EPS) * math.log2(math.e)
    row_tiles = rows // LANES
    col_tiles = cols // LANES
    half = cols // 2

    def call(body, name, out_shape, scratch, *args, limit=24, cost=None, aliases=None):
        return pl.pallas_call(
            body,
            out_shape=out_shape,
            scratch_shapes=scratch,
            compiler_params=pltpu.CompilerParams(vmem_limit_bytes=limit << 20),
            cost_estimate=cost,
            input_output_aliases=aliases or {},
            name=name,
        )(*args)

    def f32(*shape):
        return jax.ShapeDtypeStruct(shape, F32)

    row_out = f32(nx * ny, row_tiles, LANES)
    col_out = f32(nz * 2, col_tiles, LANES)
    k_shape = f32(row_tiles, cols, LANES)
    v_shape = f32(cols, LANES)
    lanes = pltpu.VMEM((cols, LANES), F32)

    def over_rows(a):
        return lax.all_to_all(a, ("x", "y"), 0, 0, tiled=True)

    def over_columns(a):
        return lax.all_to_all(a, ("z", "core"), 0, 0, tiled=True)

    blocks, columns, swapped = gather(private, generated)
    others = cols * 3 // 8
    p, t, early = call(
        functools.partial(early_score_kernel, scale),
        "early_scores",
        [
            jax.ShapeDtypeStruct((nx, 2 * ny, rows_per // 2, width), BF16),
            k_shape,
            f32(row_tiles, LANES),
        ],
        [pltpu.VMEM((cols - others, features), BF16), pltpu.VMEM((cols - others, LANES), F32)],
        *blocks, *columns,
        cost=pl.CostEstimate(
            flops=2 * (cols - others) * rows * features, bytes_accessed=24 << 20, transcendentals=0
        ),
    )
    t, lr = call(
        functools.partial(late_score_kernel, scale),
        "late_scores",
        [k_shape, row_out],
        [
            pltpu.VMEM((others, features), BF16),
            pltpu.VMEM((others, LANES), F32),
            pltpu.VMEM((row_tiles, LANES), F32),
        ],
        swapped, p, early, t,
        aliases={3: 0},
    )
    r, k, lc, base = call(
        functools.partial(first_column_kernel, math.log2(ng)),
        "first_columns",
        [f32(row_tiles, LANES), k_shape, col_out, f32(own, features)],
        [lanes, lanes],
        over_rows(lr), t, generated, noise,
    )
    k, rho, v = call(
        functools.partial(second_row_kernel, math.log2(np_)),
        "second_rows",
        [k_shape, row_out, v_shape],
        [],
        over_columns(lc), r, t, k,
        aliases={3: 0},
    )
    sums = call(
        functools.partial(column_sum_kernel, float(ng)),
        "column_sums",
        col_out,
        [lanes],
        over_rows(rho), k,
    )
    v, rho = call(
        functools.partial(row_sum_kernel, float(np_)),
        "row_sums",
        [v_shape, row_out],
        [],
        over_columns(sums), k,
    )
    rho = over_rows(rho)

    def barycenter(other):
        return call(
            functools.partial(barycenter_kernel, float(ng), other),
            "barycenter_other" if other else "barycenter_own",
            f32(half + 8, features),
            [pltpu.VMEM((half, LANES), F32), pltpu.VMEM((half, rows), BF16)],
            rho, v, k, p,
            cost=pl.CostEstimate(
                flops=2 * half * rows * features, bytes_accessed=16 << 20, transcendentals=0
            ),
        )

    theirs = swap(barycenter(True))
    mine = barycenter(False)
    parts = call(
        mean_kernel, "means", f32(nz, own * (features // LANES) + 16, LANES), [], mine, theirs
    )
    parts = lax.all_to_all(parts.astype(F16), "z", 0, 0, tiled=True).astype(F32)
    return call(update_kernel, "update", f32(own, features), [], parts, base)


def solution(mesh):
    fine = Mesh(mesh.devices.reshape(8, 4, 4, 2), ("z", "x", "y", "core"))
    in_specs = (
        P(("z", "x"), ("y", "core")),
        P(("y", "core", "z", "x"), None),
        P(("y", "core", "z", "x"), None),
    )
    out_specs = P(("y", "core", "z", "x"), None)
    return jax.shard_map(shards, mesh=fine, in_specs=in_specs, out_specs=out_specs, check_vma=False)
```

```python
import functools
import itertools
import math

import jax
import jax.numpy as jnp
from jax import lax
from jax.experimental import pallas as pl
from jax.experimental.pallas import tpu as pltpu
from jax.sharding import Mesh
from jax.sharding import PartitionSpec as P


EPS = 0.02
F32 = jnp.float32
BF16 = jnp.bfloat16
F16 = jnp.float16
LANES = 128
SUB = 64


def to_rows(column):
    flat = jnp.transpose(column)[0:1, :]
    return jnp.concatenate(
        [flat[:, q * LANES:(q + 1) * LANES] for q in range(column.shape[0] // LANES)], axis=0
    )


def sum_to_rows(lanes):
    flat = jnp.sum(jnp.transpose(lanes), axis=0, keepdims=True)
    return jnp.concatenate(
        [flat[:, q * LANES:(q + 1) * LANES] for q in range(lanes.shape[0] // LANES)], axis=0
    )


def to_columns(rows, out_ref):
    for q in range(rows.shape[0]):
        out_ref[q * LANES:(q + 1) * LANES, :] = jnp.transpose(
            jnp.broadcast_to(rows[q:q + 1, :], (LANES, LANES))
        )


def logsumexp0(x):
    top = jnp.max(x, axis=0)
    return top + jnp.log2(jnp.sum(jnp.exp2(x - top[None]), axis=0))


def chunks(n):
    return [pl.ds(c, SUB) for c in range(0, n, SUB)]


WIDE = 2 * LANES


def place(ref, pair, second, p_ref):
    nx, ny = p_ref.shape[0], p_ref.shape[1] // 2
    x, y, core = (lax.axis_index(a) for a in ("x", "y", "core"))
    for n, first in enumerate(((0, -1), (1, -2))[pair]):
        px = lax.rem(x + jnp.where(core == 0, first, second) + nx, nx)
        py = lax.rem(y + jnp.where(core == 0, second, first) + ny, ny)
        for f in range(2):
            p_ref[px, 2 * py + f] = ref[n, f]


def score_columns(scale, blocks, p_ref, t_ref, rows_ref, g_ref, c0_ref):
    nx, slices, rows, _ = p_ref.shape
    nz = 8
    z = lax.axis_index("z")
    own = blocks[0][0].shape[1]
    starts = []
    for block, k in blocks:
        pz = lax.rem(z + k + nz, nz)
        for c in range(2):
            at = pl.ds(len(starts) * own, own)
            g = block[c]
            g_ref[at, :] = g
            g = g.astype(F32)
            sq = jnp.sum(g * g, axis=1, keepdims=True)
            c0_ref[at, :] = jnp.broadcast_to(sq * (-0.5 * scale), (own, LANES))
            starts.append(pl.multiple_of((c * nz + pz) * own, own))

    def reduce(k):
        top = jnp.full((8, LANES), -jnp.inf, F32)
        for start in starts:
            t = t_ref[k, pl.ds(start, own), :]
            top = jnp.maximum(top, jnp.max(t.reshape(own // 8, 8, LANES), axis=0))
        top = jnp.max(top, axis=0, keepdims=True)
        total = jnp.zeros((8, LANES), F32)
        for start in starts:
            e = jnp.exp2(t_ref[k, pl.ds(start, own), :] - top)
            total = total + jnp.sum(e.reshape(own // 8, 8, LANES), axis=0)
        rows_ref[k:k + 1, :] = top + jnp.log2(jnp.sum(total, axis=0, keepdims=True))

    per = rows // WIDE
    for n in range(nx * per):
        at = pl.ds(n % per * WIDE, WIDE)
        p = jnp.concatenate([p_ref[n // per, f, at, :] for f in range(slices)], axis=1)
        cross = lax.dot_general(g_ref[...], p, (((1,), (1,)), ((), ())), preferred_element_type=F32)
        if n:
            reduce(2 * n - 2)
            reduce(2 * n - 1)
        for k in range(2):
            for m, start in enumerate(starts):
                part = slice(m * own, (m + 1) * own)
                t_ref[2 * n + k, pl.ds(start, own), :] = (
                    cross[part, k * LANES:(k + 1) * LANES] * scale + c0_ref[part, :]
                )
    reduce(2 * nx * per - 2)
    reduce(2 * nx * per - 1)


def early_score_kernel(scale, *refs):
    blocks, (own_ref, far_ref, near_ref) = refs[:8], refs[8:11]
    p_ref, t_ref, rows_ref, g_ref, c0_ref = refs[11:]
    for ref, pair, second in zip(blocks, (0, 1, 0, 0, 1, 1, 0, 1), (0, 0, -1, 1, -1, 1, -2, 2)):
        place(ref, pair, second, p_ref)
    sign = jnp.where(lax.axis_index("core") == 0, -1, 1)
    columns = [(own_ref, 0), (far_ref, 4)] + [(near_ref.at[k - 1], sign * k) for k in (1, 2, 3)]
    score_columns(scale, columns, p_ref, t_ref, rows_ref, g_ref, c0_ref)


def late_score_kernel(scale, swapped_ref, p_ref, early_ref, old_ref, t_ref, l_ref, g_ref, c0_ref, rows_ref):
    del old_ref
    sign = jnp.where(lax.axis_index("core") == 0, 1, -1)
    columns = [(swapped_ref.at[k - 1], sign * k) for k in (1, 2, 3)]
    score_columns(scale, columns, p_ref, t_ref, rows_ref, g_ref, c0_ref)
    late, early = rows_ref[...], early_ref[...]
    top = jnp.maximum(late, early)
    total = top + jnp.log2(jnp.exp2(late - top) + jnp.exp2(early - top))
    l_ref[...] = jnp.broadcast_to(total[None], l_ref.shape)


def first_column_kernel(log_ng, l_ref, t_ref, g_ref, n_ref, r_ref, k_ref, lc_ref, base_ref, m_ref, s_ref):
    tiles, cols, _ = t_ref.shape
    base_ref[...] = g_ref[...].astype(F32) + n_ref[...]
    r_ref[...] = log_ng - logsumexp0(l_ref[...])
    r = [r_ref[n:n + 1, :] for n in range(tiles)]

    @pl.loop(0, cols, step=SUB)
    def _(c):
        at = pl.ds(pl.multiple_of(c, SUB), SUB)
        total = jnp.zeros((SUB, LANES), F32)
        for n in range(tiles):
            e = jnp.exp2(t_ref[n, at, :] + r[n])
            k_ref[n, at, :] = e
            total = total + e
        s_ref[at, :] = total

    sums = sum_to_rows(s_ref[...])
    lc_ref[...] = jnp.broadcast_to(jnp.log2(sums)[None], lc_ref.shape)

    @pl.when(jnp.min(sums) < 1e-30)
    def _():
        @pl.loop(0, cols, step=SUB)
        def _(c):
            at = pl.ds(pl.multiple_of(c, SUB), SUB)
            top = t_ref[0, at, :] + r[0]
            for n in range(1, tiles):
                top = jnp.maximum(top, t_ref[n, at, :] + r[n])
            total = jnp.zeros((SUB, LANES), F32)
            for n in range(tiles):
                total = total + jnp.exp2(t_ref[n, at, :] + r[n] - top)
            m_ref[at, :] = top
            s_ref[at, :] = total

        m = m_ref[...]
        top = jnp.max(m, axis=1, keepdims=True)
        total = jnp.sum(s_ref[...] * jnp.exp2(m - top), axis=1, keepdims=True)
        lc = to_rows(jnp.broadcast_to(top + jnp.log2(total), m.shape))
        lc_ref[...] = jnp.broadcast_to(lc[None], lc_ref.shape)


def scaled_row_sums(k_ref, v_ref, rho_ref):
    tiles, cols, _ = k_ref.shape

    def body(i, totals):
        at = pl.ds(pl.multiple_of(i * SUB, SUB), SUB)
        v = v_ref[at, :]
        return tuple(
            totals[n] + jnp.sum((k_ref[n, at, :] * v).reshape(SUB // 8, 8, LANES), axis=0)
            for n in range(tiles)
        )

    totals = lax.fori_loop(
        0, cols // SUB, body, tuple(jnp.zeros((8, LANES), F32) for _ in range(tiles))
    )
    rho = jnp.concatenate([jnp.sum(total, axis=0, keepdims=True) for total in totals], axis=0)
    rho_ref[...] = jnp.broadcast_to(rho[None], rho_ref.shape)


def second_row_kernel(log_np, lc_ref, r_ref, t_ref, old_ref, k_ref, rho_ref, v_ref):
    del old_ref
    tiles, cols, _ = t_ref.shape
    c1 = log_np - logsumexp0(lc_ref[...])
    fits = jnp.max(c1) <= 66.0
    to_columns(jnp.where(fits, jnp.exp2(c1), c1), v_ref)

    @pl.when(jnp.logical_not(fits))
    def _():
        @pl.loop(0, cols, step=SUB)
        def _(c):
            at = pl.ds(pl.multiple_of(c, SUB), SUB)
            for n in range(tiles):
                k_ref[n, at, :] = jnp.exp2(t_ref[n, at, :] + r_ref[n:n + 1, :] + v_ref[at, :])
            v_ref[at, :] = jnp.ones((SUB, LANES), F32)

    scaled_row_sums(k_ref, v_ref, rho_ref)


def column_sum_kernel(ng, rho_ref, k_ref, sums_ref, acc_ref):
    tiles, cols, _ = k_ref.shape
    scaled = ng / jnp.sum(rho_ref[...], axis=0)
    u = [scaled[n:n + 1, :] for n in range(tiles)]

    @pl.loop(0, cols, step=SUB)
    def _(c):
        at = pl.ds(pl.multiple_of(c, SUB), SUB)
        total = k_ref[0, at, :] * u[0]
        for n in range(1, tiles):
            total = total + k_ref[n, at, :] * u[n]
        acc_ref[at, :] = total

    sums_ref[...] = jnp.broadcast_to(sum_to_rows(acc_ref[...])[None], sums_ref.shape)


def row_sum_kernel(np_, sums_ref, k_ref, v_ref, rho_ref):
    to_columns(np_ / jnp.sum(sums_ref[...], axis=0), v_ref)
    scaled_row_sums(k_ref, v_ref, rho_ref)


def barycenter_kernel(ng, other, rho_ref, v_ref, k_ref, p_ref, out_ref, mass_ref, w_ref):
    tiles = k_ref.shape[0]
    cols = mass_ref.shape[0]
    core = lax.axis_index("core")
    begin = (1 - core if other else core) * cols
    scaled = ng / jnp.sum(rho_ref[...], axis=0)
    u = [scaled[n:n + 1, :] for n in range(tiles)]

    p = jnp.concatenate(
        [
            jnp.concatenate([p_ref[x, f] for f in range(p_ref.shape[1])], axis=1)
            for x in range(p_ref.shape[0])
        ],
        axis=0,
    )
    part = cols // 2
    for first in range(0, cols, part):
        for c in range(first, first + part, SUB):
            at = pl.ds(c, SUB)
            source = pl.ds(pl.multiple_of(begin + c, SUB), SUB)
            v = v_ref[source, :]
            total = jnp.zeros((SUB, LANES), F32)
            for n in range(tiles):
                w = k_ref[n, source, :] * u[n] * v
                total = total + w
                w_ref[at, n * LANES:(n + 1) * LANES] = w.astype(BF16)
            mass_ref[at, :] = total
        out_ref[first:first + part, :] = jnp.dot(
            w_ref[first:first + part, :], p, preferred_element_type=F32
        )
    mass = jnp.sum(jnp.transpose(mass_ref[...]), axis=0, keepdims=True)
    out_ref[cols:, 0:cols] = jnp.broadcast_to(mass, (out_ref.shape[0] - cols, cols))


def mean_kernel(a_ref, b_ref, out_ref):
    owners = out_ref.shape[0]
    features = a_ref.shape[1]
    blocks = features // LANES
    rows = (out_ref.shape[1] - 16) // blocks
    cols = owners * rows
    mass = jnp.maximum(a_ref[cols:cols + 1, 0:cols] + b_ref[cols:cols + 1, 0:cols], 1e-30)
    log_mass = jnp.log2(mass)
    inverse = jnp.transpose(jnp.broadcast_to(1.0 / mass, (LANES, cols)))
    for z in range(owners):
        at = slice(z * rows, (z + 1) * rows)
        for q in range(blocks):
            lanes = slice(q * LANES, (q + 1) * LANES)
            out_ref[z, q * rows:(q + 1) * rows, :] = (a_ref[at, lanes] + b_ref[at, lanes]) * inverse[at, :]
        part = jnp.concatenate([log_mass[:, at]] * (LANES // rows), axis=1)
        high = jnp.round(part * 16.0) * 0.0625
        low = part - high
        out_ref[z, blocks * rows:, :] = jnp.concatenate([high] * 8 + [low] * 8, axis=0)


def update_kernel(parts_ref, base_ref, out_ref):
    sources = parts_ref.shape[0]
    rows = base_ref.shape[0]
    blocks = base_ref.shape[1] // LANES
    at = blocks * rows
    logs = jnp.concatenate(
        [parts_ref[d, at:at + 1, :] + parts_ref[d, at + 8:at + 9, :] for d in range(sources)], axis=0
    )
    weights = jnp.exp2(logs - jnp.max(logs, axis=0, keepdims=True))
    weights = weights / jnp.sum(weights, axis=0, keepdims=True)
    columns = [
        jnp.transpose(jnp.broadcast_to(weights[d:d + 1, :], (LANES, LANES)))[0:rows, :]
        for d in range(sources)
    ]
    for q in range(blocks):
        lanes = slice(q * LANES, (q + 1) * LANES)
        total = parts_ref[0, q * rows:(q + 1) * rows, :] * columns[0]
        for d in range(1, sources):
            total = total + parts_ref[d, q * rows:(q + 1) * rows, :] * columns[d]
        out_ref[:, lanes] = base_ref[:, lanes] - total


def permuted(a, axes, moved):
    sizes = [lax.axis_size(n) for n in axes]
    flat = lambda at: functools.reduce(lambda f, cn: f * cn[1] + cn[0] % cn[1], zip(at, sizes), 0)
    pairs = [(flat(at), flat(moved(*at))) for at in itertools.product(*map(range, sizes))]
    return lax.ppermute(a, axes, pairs)


def along(first, d, a):
    return permuted(
        a,
        ("x", "y", "core"),
        lambda x, y, c: (x + d, y, c) if (c == 0) == first else (x, y + d, c),
    )


def swap(a):
    return permuted(a, ("core",), lambda c: (1 - c,))


def gather(private, generated):
    core = lax.axis_index("core")
    rows, width = private.shape
    mine, got = private.reshape(2, rows // 2, width), swap(private).reshape(2, rows // 2, width)
    a0 = jnp.where(core == 0, jnp.stack([mine[0], got[0]]), jnp.stack([got[1], mine[1]]))
    a1, a2 = along(True, 1, a0), along(True, -1, a0)
    a3 = along(True, 2, a0)
    s = jnp.stack([a0, a1])
    s1, s2 = along(False, 1, s), along(False, -1, s)
    s, a2, a3 = lax.optimization_barrier((s, a2, a3))
    t = jnp.stack([a2, a3])
    t1, t2 = along(False, 1, t), along(False, -1, t)
    h1, h2 = along(False, 1, s1), along(False, -1, t2)

    got = swap(generated)
    g0 = jnp.where(core == 0, jnp.stack([generated, got]), jnp.stack([got, generated]))

    def onward(g, d):
        return permuted(g, ("z", "core"), lambda z, c: (z + (d if c == 0 else -d), c))

    g1, g2 = onward(g0, 1), onward(g0, 2)
    g34 = onward(jnp.stack([g1, g2]), 2)
    near, far = jnp.stack([g1, g2, g34[0]]), g34[1]
    near, far, t1, s2, h1, h2 = lax.optimization_barrier((near, far, t1, s2, h1, h2))
    return (s, t, s1, s2, t1, t2, h1, h2), (g0, far, near), swap(near)


def shards(private, generated, noise):
    rows_per, width = private.shape
    own, features = generated.shape
    nz, nx, ny = lax.axis_size("z"), lax.axis_size("x"), lax.axis_size("y")
    cols = own * nz * 2
    rows = rows_per // 2 * nx
    np_ = rows * nz * 2
    ng = cols * nx * ny
    scale = 2.0 / (features * EPS) * math.log2(math.e)
    row_tiles = rows // LANES
    col_tiles = cols // LANES
    half = cols // 2

    def call(body, name, out_shape, scratch, *args, limit=24, cost=None, aliases=None):
        return pl.pallas_call(
            body,
            out_shape=out_shape,
            scratch_shapes=scratch,
            compiler_params=pltpu.CompilerParams(vmem_limit_bytes=limit << 20),
            cost_estimate=cost,
            input_output_aliases=aliases or {},
            name=name,
        )(*args)

    def f32(*shape):
        return jax.ShapeDtypeStruct(shape, F32)

    row_out = f32(nx * ny, row_tiles, LANES)
    col_out = f32(nz * 2, col_tiles, LANES)
    k_shape = f32(row_tiles, cols, LANES)
    v_shape = f32(cols, LANES)
    lanes = pltpu.VMEM((cols, LANES), F32)

    def over_rows(a):
        return lax.all_to_all(a, ("x", "y"), 0, 0, tiled=True)

    def over_columns(a):
        return lax.all_to_all(a, ("z", "core"), 0, 0, tiled=True)

    blocks, columns, swapped = gather(private, generated)
    others = cols * 3 // 8
    p, t, early = call(
        functools.partial(early_score_kernel, scale),
        "early_scores",
        [
            jax.ShapeDtypeStruct((nx, 2 * ny, rows_per // 2, width), BF16),
            k_shape,
            f32(row_tiles, LANES),
        ],
        [pltpu.VMEM((cols - others, features), BF16), pltpu.VMEM((cols - others, LANES), F32)],
        *blocks, *columns,
        cost=pl.CostEstimate(
            flops=2 * (cols - others) * rows * features, bytes_accessed=24 << 20, transcendentals=0
        ),
    )
    t, lr = call(
        functools.partial(late_score_kernel, scale),
        "late_scores",
        [k_shape, row_out],
        [
            pltpu.VMEM((others, features), BF16),
            pltpu.VMEM((others, LANES), F32),
            pltpu.VMEM((row_tiles, LANES), F32),
        ],
        swapped, p, early, t,
        aliases={3: 0},
    )
    r, k, lc, base = call(
        functools.partial(first_column_kernel, math.log2(ng)),
        "first_columns",
        [f32(row_tiles, LANES), k_shape, col_out, f32(own, features)],
        [lanes, lanes],
        over_rows(lr), t, generated, noise,
    )
    k, rho = call(
        functools.partial(second_row_kernel, math.log2(np_)),
        "second_rows",
        [k_shape, row_out],
        [lanes],
        over_columns(lc), r, t, k,
        aliases={3: 0},
    )
    sums = call(
        functools.partial(column_sum_kernel, float(ng)),
        "column_sums",
        col_out,
        [lanes],
        over_rows(rho), k,
    )
    v, rho = call(
        functools.partial(row_sum_kernel, float(np_)),
        "row_sums",
        [v_shape, row_out],
        [],
        over_columns(sums), k,
    )
    rho = over_rows(rho)

    def barycenter(other):
        return call(
            functools.partial(barycenter_kernel, float(ng), other),
            "barycenter_other" if other else "barycenter_own",
            f32(half + 8, features),
            [pltpu.VMEM((half, LANES), F32), pltpu.VMEM((half, rows), BF16)],
            rho, v, k, p,
            cost=pl.CostEstimate(
                flops=2 * half * rows * features, bytes_accessed=16 << 20, transcendentals=0
            ),
        )

    theirs = swap(barycenter(True))
    mine = barycenter(False)
    parts = call(
        mean_kernel, "means", f32(nz, own * (features // LANES) + 16, LANES), [], mine, theirs
    )
    parts = lax.all_to_all(parts.astype(F16), "z", 0, 0, tiled=True).astype(F32)
    return call(update_kernel, "update", f32(own, features), [], parts, base)


def solution(mesh):
    fine = Mesh(mesh.devices.reshape(8, 4, 4, 2), ("z", "x", "y", "core"))
    in_specs = (
        P(("z", "x"), ("y", "core")),
        P(("y", "core", "z", "x"), None),
        P(("y", "core", "z", "x"), None),
    )
    out_specs = P(("y", "core", "z", "x"), None)
    return jax.shard_map(shards, mesh=fine, in_specs=in_specs, out_specs=out_specs, check_vma=False)
```

```python
import functools
import itertools
import math

import jax
import jax.numpy as jnp
from jax import lax
from jax.experimental import pallas as pl
from jax.experimental.pallas import tpu as pltpu
from jax.sharding import Mesh
from jax.sharding import PartitionSpec as P


EPS = 0.02
F32 = jnp.float32
BF16 = jnp.bfloat16
F16 = jnp.float16
LANES = 128
SUB = 64


def to_rows(column):
    flat = jnp.transpose(column)[0:1, :]
    return jnp.concatenate(
        [flat[:, q * LANES:(q + 1) * LANES] for q in range(column.shape[0] // LANES)], axis=0
    )


def sum_to_rows(lanes):
    flat = jnp.sum(jnp.transpose(lanes), axis=0, keepdims=True)
    return jnp.concatenate(
        [flat[:, q * LANES:(q + 1) * LANES] for q in range(lanes.shape[0] // LANES)], axis=0
    )


def to_columns(rows, out_ref):
    for q in range(rows.shape[0]):
        out_ref[q * LANES:(q + 1) * LANES, :] = jnp.transpose(
            jnp.broadcast_to(rows[q:q + 1, :], (LANES, LANES))
        )


def logsumexp0(x):
    top = jnp.max(x, axis=0)
    return top + jnp.log2(jnp.sum(jnp.exp2(x - top[None]), axis=0))


def chunks(n):
    return [pl.ds(c, SUB) for c in range(0, n, SUB)]


WIDE = 2 * LANES


def place(ref, pair, second, p_ref):
    nx, ny = p_ref.shape[0], p_ref.shape[1] // 2
    x, y, core = (lax.axis_index(a) for a in ("x", "y", "core"))
    for n, first in enumerate(((0, -1), (1, -2))[pair]):
        px = lax.rem(x + jnp.where(core == 0, first, second) + nx, nx)
        py = lax.rem(y + jnp.where(core == 0, second, first) + ny, ny)
        for f in range(2):
            p_ref[px, 2 * py + f] = ref[n, f]


def score_columns(scale, blocks, p_ref, t_ref, rows_ref, g_ref, c0_ref):
    nx, slices, rows, _ = p_ref.shape
    nz = 8
    z = lax.axis_index("z")
    own = blocks[0][0].shape[1]
    starts = []
    for block, k in blocks:
        pz = lax.rem(z + k + nz, nz)
        for c in range(2):
            at = pl.ds(len(starts) * own, own)
            g = block[c]
            g_ref[at, :] = g
            g = g.astype(F32)
            sq = jnp.sum(g * g, axis=1, keepdims=True)
            c0_ref[at, :] = jnp.broadcast_to(sq * (-0.5 * scale), (own, LANES))
            starts.append(pl.multiple_of((c * nz + pz) * own, own))

    def reduce(k):
        top = jnp.full((8, LANES), -jnp.inf, F32)
        for start in starts:
            t = t_ref[k, pl.ds(start, own), :]
            top = jnp.maximum(top, jnp.max(t.reshape(own // 8, 8, LANES), axis=0))
        top = jnp.max(top, axis=0, keepdims=True)
        total = jnp.zeros((8, LANES), F32)
        for start in starts:
            e = jnp.exp2(t_ref[k, pl.ds(start, own), :] - top)
            total = total + jnp.sum(e.reshape(own // 8, 8, LANES), axis=0)
        rows_ref[k:k + 1, :] = top + jnp.log2(jnp.sum(total, axis=0, keepdims=True))

    per = rows // WIDE
    for n in range(nx * per):
        at = pl.ds(n % per * WIDE, WIDE)
        p = jnp.concatenate([p_ref[n // per, f, at, :] for f in range(slices)], axis=1)
        cross = lax.dot_general(g_ref[...], p, (((1,), (1,)), ((), ())), preferred_element_type=F32)
        if n:
            reduce(2 * n - 2)
            reduce(2 * n - 1)
        for k in range(2):
            for m, start in enumerate(starts):
                part = slice(m * own, (m + 1) * own)
                t_ref[2 * n + k, pl.ds(start, own), :] = (
                    cross[part, k * LANES:(k + 1) * LANES] * scale + c0_ref[part, :]
                )
    reduce(2 * nx * per - 2)
    reduce(2 * nx * per - 1)


def early_score_kernel(scale, *refs):
    blocks, (own_ref, far_ref, near_ref) = refs[:8], refs[8:11]
    p_ref, t_ref, rows_ref, g_ref, c0_ref = refs[11:]
    for ref, pair, second in zip(blocks, (0, 1, 0, 0, 1, 1, 0, 1), (0, 0, -1, 1, -1, 1, -2, 2)):
        place(ref, pair, second, p_ref)
    sign = jnp.where(lax.axis_index("core") == 0, -1, 1)
    columns = [(own_ref, 0), (far_ref, 4)] + [(near_ref.at[k - 1], sign * k) for k in (1, 2, 3)]
    score_columns(scale, columns, p_ref, t_ref, rows_ref, g_ref, c0_ref)


def late_score_kernel(scale, swapped_ref, p_ref, early_ref, old_ref, t_ref, l_ref, g_ref, c0_ref, rows_ref):
    del old_ref
    sign = jnp.where(lax.axis_index("core") == 0, 1, -1)
    columns = [(swapped_ref.at[k - 1], sign * k) for k in (1, 2, 3)]
    score_columns(scale, columns, p_ref, t_ref, rows_ref, g_ref, c0_ref)
    late, early = rows_ref[...], early_ref[...]
    top = jnp.maximum(late, early)
    total = top + jnp.log2(jnp.exp2(late - top) + jnp.exp2(early - top))
    l_ref[...] = jnp.broadcast_to(total[None], l_ref.shape)


def first_column_kernel(log_ng, l_ref, t_ref, g_ref, n_ref, r_ref, k_ref, lc_ref, base_ref, m_ref, s_ref):
    tiles, cols, _ = t_ref.shape
    base_ref[...] = g_ref[...].astype(F32) + n_ref[...]
    r_ref[...] = log_ng - logsumexp0(l_ref[...])
    r = [r_ref[n:n + 1, :] for n in range(tiles)]

    @pl.loop(0, cols, step=SUB)
    def _(c):
        at = pl.ds(pl.multiple_of(c, SUB), SUB)
        total = jnp.zeros((SUB, LANES), F32)
        for n in range(tiles):
            e = jnp.exp2(t_ref[n, at, :] + r[n])
            k_ref[n, at, :] = e
            total = total + e
        s_ref[at, :] = total

    sums = sum_to_rows(s_ref[...])
    lc_ref[...] = jnp.broadcast_to(jnp.log2(sums)[None], lc_ref.shape)

    @pl.when(jnp.min(sums) < 1e-30)
    def _():
        @pl.loop(0, cols, step=SUB)
        def _(c):
            at = pl.ds(pl.multiple_of(c, SUB), SUB)
            top = t_ref[0, at, :] + r[0]
            for n in range(1, tiles):
                top = jnp.maximum(top, t_ref[n, at, :] + r[n])
            total = jnp.zeros((SUB, LANES), F32)
            for n in range(tiles):
                total = total + jnp.exp2(t_ref[n, at, :] + r[n] - top)
            m_ref[at, :] = top
            s_ref[at, :] = total

        m = m_ref[...]
        top = jnp.max(m, axis=1, keepdims=True)
        total = jnp.sum(s_ref[...] * jnp.exp2(m - top), axis=1, keepdims=True)
        lc = to_rows(jnp.broadcast_to(top + jnp.log2(total), m.shape))
        lc_ref[...] = jnp.broadcast_to(lc[None], lc_ref.shape)


def scaled_row_sums(k_ref, v_ref, rho_ref):
    tiles, cols, _ = k_ref.shape

    def body(i, totals):
        at = pl.ds(pl.multiple_of(i * SUB, SUB), SUB)
        v = v_ref[at, :]
        return tuple(
            totals[n] + jnp.sum((k_ref[n, at, :] * v).reshape(SUB // 8, 8, LANES), axis=0)
            for n in range(tiles)
        )

    totals = lax.fori_loop(
        0, cols // SUB, body, tuple(jnp.zeros((8, LANES), F32) for _ in range(tiles))
    )
    rho = jnp.concatenate([jnp.sum(total, axis=0, keepdims=True) for total in totals], axis=0)
    rho_ref[...] = jnp.broadcast_to(rho[None], rho_ref.shape)


def second_row_kernel(log_np, lc_ref, r_ref, t_ref, old_ref, k_ref, rho_ref, v_ref):
    del old_ref
    tiles, cols, _ = t_ref.shape
    c1 = log_np - logsumexp0(lc_ref[...])
    fits = jnp.max(c1) <= 66.0
    to_columns(jnp.where(fits, jnp.exp2(c1), c1), v_ref)

    @pl.when(jnp.logical_not(fits))
    def _():
        @pl.loop(0, cols, step=SUB)
        def _(c):
            at = pl.ds(pl.multiple_of(c, SUB), SUB)
            for n in range(tiles):
                k_ref[n, at, :] = jnp.exp2(t_ref[n, at, :] + r_ref[n:n + 1, :] + v_ref[at, :])
            v_ref[at, :] = jnp.ones((SUB, LANES), F32)

    scaled_row_sums(k_ref, v_ref, rho_ref)


def column_sum_kernel(ng, rho_ref, k_ref, sums_ref, acc_ref):
    tiles, cols, _ = k_ref.shape
    scaled = ng / jnp.sum(rho_ref[...], axis=0)
    u = [scaled[n:n + 1, :] for n in range(tiles)]

    @pl.loop(0, cols, step=SUB)
    def _(c):
        at = pl.ds(pl.multiple_of(c, SUB), SUB)
        total = k_ref[0, at, :] * u[0]
        for n in range(1, tiles):
            total = total + k_ref[n, at, :] * u[n]
        acc_ref[at, :] = total

    sums_ref[...] = jnp.broadcast_to(sum_to_rows(acc_ref[...])[None], sums_ref.shape)


def row_sum_kernel(np_, sums_ref, k_ref, v_ref, rho_ref):
    to_columns(np_ / jnp.sum(sums_ref[...], axis=0), v_ref)
    scaled_row_sums(k_ref, v_ref, rho_ref)


def two_parts(log_mass):
    high = jnp.round(log_mass * 16.0) * 0.0625
    return high, log_mass - high


def barycenter_kernel(ng, other, rho_ref, v_ref, k_ref, p_ref, out_ref, mass_ref, w_ref):
    tiles = k_ref.shape[0]
    cols = mass_ref.shape[0]
    core = lax.axis_index("core")
    begin = (1 - core if other else core) * cols
    scaled = ng / jnp.sum(rho_ref[...], axis=0)
    u = [scaled[n:n + 1, :] for n in range(tiles)]

    p = jnp.concatenate(
        [
            jnp.concatenate([p_ref[x, f] for f in range(p_ref.shape[1])], axis=1)
            for x in range(p_ref.shape[0])
        ],
        axis=0,
    )
    part = cols // 2
    for first in range(0, cols, part):
        for c in range(first, first + part, SUB):
            at = pl.ds(c, SUB)
            source = pl.ds(pl.multiple_of(begin + c, SUB), SUB)
            v = v_ref[source, :]
            total = jnp.zeros((SUB, LANES), F32)
            for n in range(tiles):
                w = k_ref[n, source, :] * u[n] * v
                total = total + w
                w_ref[at, n * LANES:(n + 1) * LANES] = w.astype(BF16)
            mass_ref[at, :] = total
        sums = jnp.dot(w_ref[first:first + part, :], p, preferred_element_type=F32)
        if other:
            weight = jnp.sum(mass_ref[first:first + part, :], axis=1, keepdims=True)
            sums = sums * (1.0 / jnp.maximum(weight, 1e-30))
        out_ref[first:first + part, :] = sums
    mass = jnp.sum(jnp.transpose(mass_ref[...]), axis=0, keepdims=True)
    if other:
        high, low = two_parts(jnp.log2(jnp.maximum(mass, 1e-30)))
        mass = jnp.concatenate([high] * 4 + [low] * 4, axis=0)
    mass = jnp.broadcast_to(mass, (out_ref.shape[0] - cols, cols))
    out_ref[cols:, :] = jnp.concatenate([mass] * (out_ref.shape[1] // cols), axis=1)


def mean_kernel(a_ref, b_ref, out_ref):
    owners = out_ref.shape[0]
    features = a_ref.shape[1]
    blocks = features // LANES
    rows = (out_ref.shape[1] - 16) // blocks
    cols = owners * rows
    other = jnp.exp2(b_ref[cols:cols + 1, 0:cols] + b_ref[cols + 4:cols + 5, 0:cols])
    mass = jnp.maximum(a_ref[cols:cols + 1, 0:cols] + other, 1e-30)
    log_mass = jnp.log2(mass)
    inverse = jnp.transpose(jnp.broadcast_to(1.0 / mass, (LANES, cols)))
    share = jnp.transpose(jnp.broadcast_to(other / mass, (LANES, cols)))
    for z in range(owners):
        at = slice(z * rows, (z + 1) * rows)
        for q in range(blocks):
            lanes = slice(q * LANES, (q + 1) * LANES)
            out_ref[z, q * rows:(q + 1) * rows, :] = (
                a_ref[at, lanes] * inverse[at, :] + b_ref[at, lanes] * share[at, :]
            )
        high, low = two_parts(jnp.concatenate([log_mass[:, at]] * (LANES // rows), axis=1))
        out_ref[z, blocks * rows:, :] = jnp.concatenate([high] * 8 + [low] * 8, axis=0)


def update_kernel(parts_ref, base_ref, out_ref):
    sources = parts_ref.shape[0]
    rows = base_ref.shape[0]
    blocks = base_ref.shape[1] // LANES
    at = blocks * rows
    logs = jnp.concatenate(
        [parts_ref[d, at:at + 1, :] + parts_ref[d, at + 8:at + 9, :] for d in range(sources)], axis=0
    )
    weights = jnp.exp2(logs - jnp.max(logs, axis=0, keepdims=True))
    weights = weights / jnp.sum(weights, axis=0, keepdims=True)
    columns = [
        jnp.transpose(jnp.broadcast_to(weights[d:d + 1, :], (LANES, LANES)))[0:rows, :]
        for d in range(sources)
    ]
    for q in range(blocks):
        lanes = slice(q * LANES, (q + 1) * LANES)
        total = parts_ref[0, q * rows:(q + 1) * rows, :] * columns[0]
        for d in range(1, sources):
            total = total + parts_ref[d, q * rows:(q + 1) * rows, :] * columns[d]
        out_ref[:, lanes] = base_ref[:, lanes] - total


def permuted(a, axes, moved):
    sizes = [lax.axis_size(n) for n in axes]
    flat = lambda at: functools.reduce(lambda f, cn: f * cn[1] + cn[0] % cn[1], zip(at, sizes), 0)
    pairs = [(flat(at), flat(moved(*at))) for at in itertools.product(*map(range, sizes))]
    return lax.ppermute(a, axes, pairs)


def along(first, d, a):
    return permuted(
        a,
        ("x", "y", "core"),
        lambda x, y, c: (x + d, y, c) if (c == 0) == first else (x, y + d, c),
    )


def swap(a):
    return permuted(a, ("core",), lambda c: (1 - c,))


def gather(private, generated):
    core = lax.axis_index("core")
    rows, width = private.shape
    mine, got = private.reshape(2, rows // 2, width), swap(private).reshape(2, rows // 2, width)
    a0 = jnp.where(core == 0, jnp.stack([mine[0], got[0]]), jnp.stack([got[1], mine[1]]))
    a1, a2 = along(True, 1, a0), along(True, -1, a0)
    a3 = along(True, 2, a0)
    s = jnp.stack([a0, a1])
    s1, s2 = along(False, 1, s), along(False, -1, s)
    s, a2, a3 = lax.optimization_barrier((s, a2, a3))
    t = jnp.stack([a2, a3])
    t1, t2 = along(False, 1, t), along(False, -1, t)
    h1, h2 = along(False, 1, s1), along(False, -1, t2)

    got = swap(generated)
    g0 = jnp.where(core == 0, jnp.stack([generated, got]), jnp.stack([got, generated]))

    def onward(g, d):
        return permuted(g, ("z", "core"), lambda z, c: (z + (d if c == 0 else -d), c))

    g1, g2 = onward(g0, 1), onward(g0, 2)
    g34 = onward(jnp.stack([g1, g2]), 2)
    near, far = jnp.stack([g1, g2, g34[0]]), g34[1]
    near, far, t1, s2, h1, h2 = lax.optimization_barrier((near, far, t1, s2, h1, h2))
    return (s, t, s1, s2, t1, t2, h1, h2), (g0, far, near), swap(near)


def shards(private, generated, noise):
    rows_per, width = private.shape
    own, features = generated.shape
    nz, nx, ny = lax.axis_size("z"), lax.axis_size("x"), lax.axis_size("y")
    cols = own * nz * 2
    rows = rows_per // 2 * nx
    np_ = rows * nz * 2
    ng = cols * nx * ny
    scale = 2.0 / (features * EPS) * math.log2(math.e)
    row_tiles = rows // LANES
    col_tiles = cols // LANES
    half = cols // 2

    def call(body, name, out_shape, scratch, *args, limit=24, cost=None, aliases=None):
        return pl.pallas_call(
            body,
            out_shape=out_shape,
            scratch_shapes=scratch,
            compiler_params=pltpu.CompilerParams(vmem_limit_bytes=limit << 20),
            cost_estimate=cost,
            input_output_aliases=aliases or {},
            name=name,
        )(*args)

    def f32(*shape):
        return jax.ShapeDtypeStruct(shape, F32)

    row_out = f32(nx * ny, row_tiles, LANES)
    col_out = f32(nz * 2, col_tiles, LANES)
    k_shape = f32(row_tiles, cols, LANES)
    v_shape = f32(cols, LANES)
    lanes = pltpu.VMEM((cols, LANES), F32)

    def over_rows(a):
        return lax.all_to_all(a, ("x", "y"), 0, 0, tiled=True)

    def over_columns(a):
        return lax.all_to_all(a, ("z", "core"), 0, 0, tiled=True)

    blocks, columns, swapped = gather(private, generated)
    others = cols * 3 // 8
    p, t, early = call(
        functools.partial(early_score_kernel, scale),
        "early_scores",
        [
            jax.ShapeDtypeStruct((nx, 2 * ny, rows_per // 2, width), BF16),
            k_shape,
            f32(row_tiles, LANES),
        ],
        [pltpu.VMEM((cols - others, features), BF16), pltpu.VMEM((cols - others, LANES), F32)],
        *blocks, *columns,
        cost=pl.CostEstimate(
            flops=2 * (cols - others) * rows * features, bytes_accessed=24 << 20, transcendentals=0
        ),
    )
    t, lr = call(
        functools.partial(late_score_kernel, scale),
        "late_scores",
        [k_shape, row_out],
        [
            pltpu.VMEM((others, features), BF16),
            pltpu.VMEM((others, LANES), F32),
            pltpu.VMEM((row_tiles, LANES), F32),
        ],
        swapped, p, early, t,
        aliases={3: 0},
    )
    r, k, lc, base = call(
        functools.partial(first_column_kernel, math.log2(ng)),
        "first_columns",
        [f32(row_tiles, LANES), k_shape, col_out, f32(own, features)],
        [lanes, lanes],
        over_rows(lr), t, generated, noise,
    )
    k, rho = call(
        functools.partial(second_row_kernel, math.log2(np_)),
        "second_rows",
        [k_shape, row_out],
        [lanes],
        over_columns(lc), r, t, k,
        aliases={3: 0},
    )
    sums = call(
        functools.partial(column_sum_kernel, float(ng)),
        "column_sums",
        col_out,
        [lanes],
        over_rows(rho), k,
    )
    v, rho = call(
        functools.partial(row_sum_kernel, float(np_)),
        "row_sums",
        [v_shape, row_out],
        [],
        over_columns(sums), k,
    )
    rho = over_rows(rho)

    def barycenter(other):
        return call(
            functools.partial(barycenter_kernel, float(ng), other),
            "barycenter_other" if other else "barycenter_own",
            f32(half + 8, features),
            [pltpu.VMEM((half, LANES), F32), pltpu.VMEM((half, rows), BF16)],
            rho, v, k, p,
            cost=pl.CostEstimate(
                flops=2 * half * rows * features, bytes_accessed=16 << 20, transcendentals=0
            ),
        )

    theirs = swap(barycenter(True).astype(F16)).astype(F32)
    mine = barycenter(False)
    parts = call(
        mean_kernel, "means", f32(nz, own * (features // LANES) + 16, LANES), [], mine, theirs
    )
    parts = lax.all_to_all(parts.astype(F16), "z", 0, 0, tiled=True).astype(F32)
    return call(update_kernel, "update", f32(own, features), [], parts, base)


def solution(mesh):
    fine = Mesh(mesh.devices.reshape(8, 4, 4, 2), ("z", "x", "y", "core"))
    in_specs = (
        P(("z", "x"), ("y", "core")),
        P(("y", "core", "z", "x"), None),
        P(("y", "core", "z", "x"), None),
    )
    out_specs = P(("y", "core", "z", "x"), None)
    return jax.shard_map(shards, mesh=fine, in_specs=in_specs, out_specs=out_specs, check_vma=False)
```
